256 devices in a mesh: col: 32 (over y, z), lay: 8 (over x, core).
Axes of the slice: x: 4, y: 4, z: 8, core: 2. Of those that a mesh axis runs over, the one named last changes fastest.
Arguments:
- flux_operator: bfloat16 [32, 8, 4, 1024, 1024], P('col', 'lay'), as said below
- dof_order: int32 [32, 8, 1024], P('col', 'lay'), may hold values from 0 to 1023, each once within a row
- local_gap: float32 [32, 8, 4, 1024, 128], P('col', 'lay'), may hold values from -6 to 6
- rigid_load: float32 [32, 8, 4, 128], P('col', 'lay'), may hold values from -96 to 96
Outputs:
- multipliers: float32 [32, 8, 4, 1024, 128], P('col', 'lay')
The draws below stay inside these ranges and needn't reach their ends.
Inputs may be any that keep to these rules, and one draw needn't show every extreme that they name: `flux_operator`: each subdomain's operator of each species is symmetric positive definite.
All inputs are finite; a program needn't handle non-finite values.
Results may differ from the reference program's by a relative error of at most 0.0005.
The reference program's roundings to bfloat16 on the way count: a program that leaves them out, or rounds other values in their place, can miss the bound.
Values sent between devices are 32-bit elements; how exact they have to be, the bound alone decides.
No kernel may reach another device: no remote copies, remote signals or barrier semaphores. Data moves between devices by JAX's collectives and lax.ppermute only.
A program may use at most 128 MiB of HBM per device.

```python
import math
import jax
import jax.numpy as jnp
from jax import lax

FACE_SIDE = 192
FACE_TOP = 128
SPECIES = 4
CASES = 128
YCOLS = 4
ITERS = 3
M = 1024
NCOLS = 32
NLAYS = 8
N_COL = 32
N_LAY = 8


def draw_flux_operator(key, part):
    key = jax.random.fold_in(key, 7)
    noise_key, diag_key = jax.random.split(key)
    shape = (NCOLS, NLAYS, SPECIES, M, M)
    noise = jax.random.normal(noise_key, shape, jnp.float32)
    diag = jax.random.uniform(diag_key, (NCOLS, NLAYS, SPECIES, M), jnp.float32, 1.0, 3.0)
    sym = (noise + jnp.swapaxes(noise, -1, -2)) * (0.3 / math.sqrt(2.0 * M))
    rows = jnp.arange(M)
    eye = rows[:, None] == rows[None, :]
    full = sym + jnp.where(eye, diag[..., None], 0.0)
    return full.astype(jnp.bfloat16)


def level_of(key, dims, pieces, smallest, largest):
    def one(position, parts):
        heights = jax.random.uniform(jax.random.fold_in(jax.random.fold_in(key, 6), position), (parts,), jnp.float32, smallest / len(pieces), largest / len(pieces))
        return jnp.repeat(jnp.exp(heights), dims[position] // parts).reshape((-1,) + (1,) * (len(dims) - position - 1))

    level = one(*pieces[0])
    for cut in pieces[1:]:
        level = level * one(*cut)
    return level


def bell_draw(own_key, shape, deviation, limit, cuts=(), kind=jnp.bfloat16):
    array = deviation * jax.random.normal(own_key, shape, jnp.float32)
    if cuts:
        array = array * level_of(own_key, shape, cuts, -0.22, 0.18)
    return jnp.clip(array, -limit, limit).astype(kind)


def setup_inputs(seed: int = 0) -> dict:
    arg_keys = jax.random.split(jax.random.key(seed), 5)
    flux_operator = draw_flux_operator(jax.random.fold_in(arg_keys[4], 71), 0)
    dof_order = jax.vmap(lambda own: jax.random.permutation(own, M))(jax.random.split(arg_keys[1], NCOLS * NLAYS)).reshape((NCOLS, NLAYS, M)).astype(jnp.int32)
    local_gap = bell_draw(arg_keys[2], (NCOLS, NLAYS, SPECIES, M, CASES), 1.0, 6.0, ((0, 32), (1, 8)), jnp.float32)
    rigid_load = bell_draw(arg_keys[3], (NCOLS, NLAYS, SPECIES, CASES), 16.0, 96.0, ((0, 32), (1, 8)), jnp.float32)
    return dict(flux_operator=flux_operator, dof_order=dof_order, local_gap=local_gap, rigid_load=rigid_load)


def coarse_matrix(xcount, ycount, zcount, side, top):
    count = xcount * ycount * zcount
    index = jnp.arange(count)
    zpos = index % zcount
    cpos = index // zcount
    ypos = cpos % ycount
    xpos = cpos // ycount
    dx = jnp.abs(xpos[:, None] - xpos[None, :])
    dy = jnp.abs(ypos[:, None] - ypos[None, :])
    dz = jnp.abs(zpos[:, None] - zpos[None, :])
    lateral = (dx == 1) & (dy == 0) & (dz == 0) | (dx == 0) & (dy == 1) & (dz == 0)
    upward = (dx == 0) & (dy == 0) & (dz == 1)
    width = 4 * side + 2 * top
    matrix = width * jnp.eye(count, dtype=jnp.float32)
    matrix = matrix - side * lateral.astype(jnp.float32) - top * upward.astype(jnp.float32)
    return matrix

def coarse_solve(chol, rhs):
    count = chol.shape[0]
    flat = rhs.reshape(count, -1)
    inner_z = lax.linalg.triangular_solve(chol, flat, left_side=True, lower=True)
    result = lax.linalg.triangular_solve(chol, inner_z, left_side=True, lower=True, transpose_a=True)
    return result.reshape(rhs.shape)

def from_next(block, axis):
    count = block.shape[axis]
    rest = lax.slice_in_dim(block, 1, count, axis=axis)
    zero = jnp.zeros_like(lax.slice_in_dim(block, 0, 1, axis=axis))
    return jnp.concatenate([rest, zero], axis=axis)

def from_prev(block, axis):
    count = block.shape[axis]
    rest = lax.slice_in_dim(block, 0, count - 1, axis=axis)
    zero = jnp.zeros_like(lax.slice_in_dim(block, 0, 1, axis=axis))
    return jnp.concatenate([zero, rest], axis=axis)

def reference(flux_operator, dof_order, local_gap, rigid_load):
    xcount = N_COL // YCOLS
    nlay = N_LAY
    count = N_COL * N_LAY
    sizes = [FACE_SIDE, FACE_SIDE, FACE_SIDE, FACE_SIDE, FACE_TOP, FACE_TOP]
    starts = [0]
    for size in sizes:
        starts.append(starts[-1] + size)
    grid = (xcount, YCOLS, nlay)
    gap = local_gap.reshape(grid + (SPECIES, M, CASES))
    load = rigid_load.reshape(grid + (SPECIES, CASES))

    def split(field):
        return [field[..., starts[f]:starts[f + 1], :] for f in range(6)]

    def assemble(field):
        xm, xp, ym, yp, zm, zp = split(field)
        return jnp.concatenate([xm - from_prev(xp, 0), xp - from_next(xm, 0), ym - from_prev(yp, 1), yp - from_next(ym, 1), zm - from_prev(zp, 2), zp - from_next(zm, 2)], axis=4)
    ones = jnp.ones(grid, jnp.float32)
    flags = [from_prev(ones, 0), from_next(ones, 0), from_prev(ones, 1), from_next(ones, 1), from_prev(ones, 2), from_next(ones, 2)]
    weight = jnp.concatenate([jnp.broadcast_to((1.0 - 0.5 * flags[f])[:, :, :, None, None, None], grid + (1, sizes[f], 1)) for f in range(6)], axis=4)

    def inner(left, right):
        return jnp.sum(weight * left * right, axis=(0, 1, 2, 4))

    def spread(coarse_y):
        values = [coarse_y - from_prev(coarse_y, 0), coarse_y - from_next(coarse_y, 0), coarse_y - from_prev(coarse_y, 1), coarse_y - from_next(coarse_y, 1), coarse_y - from_prev(coarse_y, 2), coarse_y - from_next(coarse_y, 2)]
        return jnp.concatenate([jnp.broadcast_to(values[f][:, :, :, :, None, :], grid + (SPECIES, sizes[f], CASES)) for f in range(6)], axis=4)
    chol = jnp.linalg.cholesky(coarse_matrix(xcount, YCOLS, nlay, FACE_SIDE, FACE_TOP))

    def solve(rhs):
        return coarse_solve(chol, rhs.reshape((count, SPECIES, CASES))).reshape(grid + (SPECIES, CASES))
    flux_flat = flux_operator.reshape(count, SPECIES, M, M)
    order_flat = dof_order.reshape(count, M)

    def apply_one(items):
        flux, order, field = items
        local = field[:, order, :].astype(jnp.bfloat16).astype(jnp.float32)
        image = jnp.einsum('kij,kjn->kin', flux.astype(jnp.float32), local)
        return jnp.zeros_like(image).at[:, order, :].set(image)

    def apply(field):
        flat = field.reshape(count, SPECIES, M, CASES)
        return lax.map(apply_one, (flux_flat, order_flat, flat)).reshape(field.shape)

    def project(resid):
        return resid - spread(solve(jnp.sum(resid, axis=4)))
    multipliers = spread(solve(load))
    resid = assemble(gap - apply(multipliers))
    projected = project(resid)
    energy = inner(projected, projected)
    direction = projected
    for step in range(ITERS):
        image = assemble(apply(direction))
        alpha = energy / inner(direction, image)
        multipliers = multipliers + alpha[:, None, :] * direction
        if step + 1 < ITERS:
            resid = resid - alpha[:, None, :] * image
            projected = project(resid)
            new_energy = inner(projected, projected)
            direction = projected + (new_energy / energy)[:, None, :] * direction
            energy = new_energy
    return multipliers.reshape(N_COL, N_LAY, SPECIES, M, CASES)
```

```python
import functools

import jax
import jax.numpy as jnp
import numpy as np
from jax import lax
from jax.experimental import pallas as pl
from jax.experimental.pallas import tpu as pltpu
from jax.sharding import PartitionSpec as P

SIDE = 192
TOP = 128
YCOLS = 4
SPECIES = 4
CASES = 128
M = 1024
NCOL = 32
NLAY = 8
COUNT = NCOL * NLAY
SIZES = (SIDE, SIDE, SIDE, SIDE, TOP, TOP)
STARTS = (0, 192, 384, 576, 768, 896)
TAILS = (16, 16, 16, 16, 8, 8)
CHUNK = 256
F32 = jnp.float32
BF16 = jnp.bfloat16
VMEM_LIMIT = 44 * 1024 * 1024


def coarse_inverse():
    index = np.arange(COUNT)
    zpos, cpos = index % NLAY, index // NLAY
    ypos, xpos = cpos % YCOLS, cpos // YCOLS
    dx = np.abs(xpos[:, None] - xpos[None, :])
    dy = np.abs(ypos[:, None] - ypos[None, :])
    dz = np.abs(zpos[:, None] - zpos[None, :])
    lateral = (dx + dy == 1) & (dz == 0)
    upward = (dx + dy == 0) & (dz == 1)
    matrix = M * np.eye(COUNT) - SIDE * lateral - TOP * upward
    return np.linalg.inv(matrix).astype(np.float32)


def params():
    return pltpu.CompilerParams(
        dimension_semantics=("arbitrary",), vmem_limit_bytes=VMEM_LIMIT
    )


def cost(flops, nbytes):
    return pl.CostEstimate(flops=int(flops), bytes_accessed=int(nbytes), transcendentals=0)


SMEM = pl.BlockSpec(memory_space=pltpu.SMEM)


def per_species(*shape):
    zeros = (0,) * len(shape)
    return pl.BlockSpec((1,) + shape, lambda k: (k,) + zeros)


def whole(*shape):
    zeros = (0,) * len(shape)
    return pl.BlockSpec(shape, lambda k: zeros)


def even(*shape):
    zeros = (0,) * len(shape)
    return pl.BlockSpec((1,) + shape, lambda k: (2 * k,) + zeros)


def pair(*shape):
    zeros = (0,) * len(shape)
    return pl.BlockSpec((2,) + shape, lambda k: (k,) + zeros)


def out(shape, dtype=F32):
    return jax.ShapeDtypeStruct(shape, dtype)


def exact_dot(a, b, dims):
    return lax.dot_general(
        a, b, (dims, ((), ())), precision=lax.Precision.HIGHEST, preferred_element_type=F32
    )


def prep_kernel(row_ref, col_ref, flux_ref, gap_ref, load_ref, *outs):
    o_ref, ot_ref, rt_ref, msg_ref = outs[:4]
    face_refs = outs[4:]
    row = row_ref[...]

    @pl.when(pl.program_id(0) == 0)
    def _():
        for i in range(0, M, CHUNK):
            lanes = lax.broadcasted_iota(jnp.int32, (CHUNK, M), 1)
            hit = col_ref[i : i + CHUNK, :] == lanes
            o_ref[i : i + CHUNK, :] = jnp.where(hit, 1.0, 0.0).astype(BF16)
            rows = lax.broadcasted_iota(jnp.int32, (CHUNK, M), 0) + i
            ot_ref[i : i + CHUNK, :] = jnp.where(row == rows, 1.0, 0.0).astype(BF16)

    face = lax.broadcasted_iota(jnp.int32, (16, M), 0)
    low = jnp.where(face <= 4, SIDE * face, jnp.where(face == 5, STARTS[5], M))
    high = jnp.where(face <= 3, SIDE * (face + 1), jnp.where(face == 4, STARTS[5], M))
    member = jnp.where((row >= low) & (row < high), 1.0, 0.0).astype(BF16)
    sums = lax.dot_general(
        member, flux_ref[0], (((1,), (1,)), ((), ())), preferred_element_type=F32
    )
    first = sums.astype(BF16)
    rest = sums - first.astype(F32)
    second = rest.astype(BF16)
    third = (rest - second.astype(F32)).astype(BF16)
    o = o_ref[...]
    rt = jnp.dot(first, o, preferred_element_type=F32)
    rt = rt + jnp.dot(second, o, preferred_element_type=F32)
    rt = rt + jnp.dot(third, o, preferred_element_type=F32)
    rt = rt[:8]
    rt_ref[0] = rt

    lane = lax.broadcasted_iota(jnp.int32, (8, M), 1)
    slot = lax.broadcasted_iota(jnp.int32, (8, CASES), 1)
    peer = lax.broadcasted_iota(jnp.int32, (8, CASES), 0)
    table = jnp.zeros((8, CASES), F32)
    for f in range(6):
        inside = (lane >= STARTS[f]) & (lane < STARTS[f] + SIZES[f])
        total = jnp.sum(jnp.where(inside, rt, 0.0), axis=1, keepdims=True)
        here = (slot == 6 * f + peer) & (peer < 6)
        table = table + jnp.where(here, total, 0.0)
    rows = [
        jnp.sum(gap_ref[0, STARTS[f] : STARTS[f] + SIZES[f], :], axis=0, keepdims=True)
        for f in range(6)
    ]
    rows.append(load_ref[0])
    rows.append(jnp.sum(table, axis=0, keepdims=True))
    for r in range(8):
        msg_ref[0, r : r + 1, :] = rows[r]
        msg_ref[1, r : r + 1, :] = rows[r]

    for f in range(6):
        size = SIZES[f]
        face_refs[f][0, :size, :] = gap_ref[0, STARTS[f] : STARTS[f] + size, :]
        turned = rt if STARTS[f] == 0 else pltpu.roll(rt, M - STARTS[f], 1)
        face_refs[f][0, size : size + 8, :] = turned[:, :CASES]
        if size > CASES:
            face_refs[f][0, size + 8 : size + 16, :] = turned[:, CASES : 2 * CASES]


def prep(order, flux, gap, load):
    faces = [(SPECIES, SIZES[f] + TAILS[f], CASES) for f in range(6)]
    return pl.pallas_call(
        prep_kernel,
        grid=(SPECIES,),
        in_specs=[
            whole(1, M),
            whole(M, 1),
            per_species(M, M),
            per_species(M, CASES),
            per_species(1, CASES),
        ],
        out_specs=[whole(M, M), whole(M, M), per_species(8, M), pair(8, CASES)]
        + [per_species(*shape[1:]) for shape in faces],
        out_shape=[
            out((M, M), BF16),
            out((M, M), BF16),
            out((SPECIES, 8, M)),
            out((8, 8, CASES)),
        ]
        + [out(shape) for shape in faces],
        compiler_params=params(),
        cost_estimate=cost(1e9, 20e6),
        name="prep",
    )(order.reshape(1, M), order.reshape(M, 1), flux, gap, load.reshape(SPECIES, 1, CASES))


def shifted(value, f):
    row = lax.broadcasted_iota(jnp.int32, value.shape, 0)
    zpos = row % NLAY
    ypos = (row // NLAY) % YCOLS
    xpos = row // (NLAY * YCOLS)
    step, ok = (
        (NLAY * YCOLS, xpos > 0),
        (-NLAY * YCOLS, xpos < NCOL // YCOLS - 1),
        (NLAY, ypos > 0),
        (-NLAY, ypos < YCOLS - 1),
        (1, zpos > 0),
        (-1, zpos < NLAY - 1),
    )[f]
    return jnp.where(ok, pltpu.roll(value, step % COUNT, 0), 0.0)


def solve0_kernel(info_ref, inv_ref, gathered_ref, out_ref, vals_ref):
    col = info_ref[0]

    def rows(r):
        return gathered_ref[:, r].reshape(COUNT, CASES)

    inv = inv_ref[...]
    y0 = exact_dot(inv, rows(6), ((1,), (0,)))
    vals = [y0 - shifted(y0, f) for f in range(6)]
    rounded = [v.astype(BF16).astype(F32) for v in vals]
    table = rows(7)
    tau = []
    for f in range(6):
        total = rows(f)
        for g in range(6):
            total = total - table[:, 6 * f + g : 6 * f + g + 1] * rounded[g]
        tau.append(total)
    h = jnp.zeros((COUNT, CASES), F32)
    for f in range(6):
        h = h + (tau[f] - shifted(tau[f ^ 1], f))
    y1 = exact_dot(inv, h, ((1,), (0,)))
    here = pl.ds(pl.multiple_of(col * NLAY, NLAY), NLAY)
    zero = jnp.zeros((NLAY, CASES), F32)
    for f in range(6):
        vals_ref[0] = y1 - shifted(y1, f)
        out_ref[:, f, :] = vals_ref[0, here, :]
    for f in range(6):
        vals_ref[f] = vals[f]
    for g in range(6):
        out_ref[:, 8 + g, :] = vals_ref[g, here, :]
    for f in range(4):
        away = jnp.clip(col + (-YCOLS, YCOLS, -1, 1)[f], 0, NCOL - 1)
        there = pl.ds(pl.multiple_of(away * NLAY, NLAY), NLAY)
        for g in range(6):
            out_ref[:, 16 + 8 * f + g, :] = vals_ref[g, there, :]
    for f in (4, 5):
        for g in range(6):
            out_ref[:, 16 + 8 * f + g, :] = pltpu.roll(
                vals_ref[g, here, :], (1, NLAY - 1)[f - 4], 0
            )
    for group in range(8):
        out_ref[:, 8 * group + 6, :] = zero
        out_ref[:, 8 * group + 7, :] = zero


def solve0(info, inverse, gathered):
    return pl.pallas_call(
        solve0_kernel,
        in_specs=[SMEM, pl.BlockSpec(memory_space=pltpu.VMEM), pl.BlockSpec(memory_space=pltpu.VMEM)],
        out_specs=pl.BlockSpec(memory_space=pltpu.VMEM),
        out_shape=out((8, 64, CASES)),
        scratch_shapes=[pltpu.VMEM((6, COUNT, CASES), F32)],
        compiler_params=pltpu.CompilerParams(vmem_limit_bytes=VMEM_LIMIT),
        cost_estimate=cost(1e8, 2e6),
        name="solve_start",
    )(info, inverse, gathered)


def mid_kernel(got_ref, out_ref):
    total = got_ref[0]
    top = got_ref[0, 5:6, :]
    for l in range(1, NLAY):
        total = total + got_ref[l]
        top = jnp.maximum(top, got_ref[l, 5:6, :])
    qq = jnp.zeros((1, CASES), F32)
    for l in range(NLAY):
        part = got_ref[l, 5:6, :] / top
        qq = qq + got_ref[l, 2:3, :] * (part * part)
    row = lax.broadcasted_iota(jnp.int32, (8, CASES), 0)
    dots = jnp.where(row == 2, qq, jnp.where(row == 5, top, total))
    heads = jnp.concatenate([got_ref[l, 0:1, :] for l in range(NLAY)], axis=0)
    for c in range(NCOL):
        out_ref[c, 0:8, :] = heads
        out_ref[c, 8:16, :] = dots


def mid(got):
    return pl.pallas_call(
        mid_kernel,
        in_specs=[pl.BlockSpec(memory_space=pltpu.VMEM)],
        out_specs=pl.BlockSpec(memory_space=pltpu.VMEM),
        out_shape=out((NCOL, 16, CASES)),
        cost_estimate=cost(1e5, 3e5),
        name="combine_layers",
    )(got)


def solve_kernel(info_ref, inv_ref, gathered_ref, out_ref, y_ref):
    col = info_ref[0]
    dots = jnp.sum(gathered_ref[:, 8:16, :], axis=0)
    tops = gathered_ref[:, 13, :]
    top = jnp.max(tops, axis=0, keepdims=True)
    part = tops / top
    qq = jnp.sum(gathered_ref[:, 10, :] * (part * part), axis=0, keepdims=True)
    h = gathered_ref[:, 0:8, :].reshape(COUNT, CASES) / top
    y = exact_dot(inv_ref[...], h, ((1,), (0,)))
    hy = jnp.sum(h * y, axis=0, keepdims=True)
    pq, wq, energy = dots[1:2], dots[3:4], dots[4:5]
    alpha = energy / pq
    scaled = alpha * top
    new = energy - 2.0 * (alpha * wq) + (scaled * scaled) * (qq - hy)
    beta = new / energy
    y = y * top
    here = pl.ds(pl.multiple_of(col * NLAY, NLAY), NLAY)
    for f in range(6):
        y_ref[...] = y - shifted(y, f)
        out_ref[:, f, :] = y_ref[here, :]
    out_ref[:, 6, :] = jnp.broadcast_to(alpha, (NLAY, CASES))
    out_ref[:, 7, :] = jnp.broadcast_to(beta, (NLAY, CASES))


def solve(info, inverse, gathered):
    return pl.pallas_call(
        solve_kernel,
        in_specs=[SMEM, pl.BlockSpec(memory_space=pltpu.VMEM), pl.BlockSpec(memory_space=pltpu.VMEM)],
        out_specs=pl.BlockSpec(memory_space=pltpu.VMEM),
        out_shape=out((8, 8, CASES)),
        scratch_shapes=[pltpu.VMEM((COUNT, CASES), F32)],
        cost_estimate=cost(1e8, 1e6),
        name="solve_step",
    )(info, inverse, gathered)


def apply_to(vector, o_ref, ot_ref, flux_ref, first_ref, second_ref):
    first_ref[...] = vector.astype(BF16)

    def gather(i, _):
        here = pl.ds(pl.multiple_of(i * CHUNK, CHUNK), CHUNK)
        moved = jnp.dot(o_ref[here, :], first_ref[...], preferred_element_type=F32)
        second_ref[here, :CASES] = moved.astype(BF16)
        return 0

    lax.fori_loop(0, M // CHUNK, gather, 0)
    first_ref[...] = second_ref[:, :CASES]

    def image(i, _):
        here = pl.ds(pl.multiple_of(i * CHUNK, CHUNK), CHUNK)
        part = jnp.dot(flux_ref[0, here, :], first_ref[...], preferred_element_type=F32)
        high = part.astype(BF16)
        second_ref[here, :CASES] = high
        second_ref[here, CASES:] = (part - high.astype(F32)).astype(BF16)
        return 0

    lax.fori_loop(0, M // CHUNK, image, 0)

    def back(start, size):
        both = jnp.dot(
            ot_ref[start : start + size, :], second_ref[...], preferred_element_type=F32
        )
        return both[:, :CASES] + both[:, CASES:]

    return back


def start_kernel(gap_ref, rt_ref, back_ref, o_ref, ot_ref, flux_ref, *refs):
    arrived = refs[:6]
    p_ref = refs[6]
    faces = refs[7:13]
    first_ref, second_ref = refs[13:]
    mine = back_ref[0, 8:16, :].astype(BF16).astype(F32)
    own = exact_dot(rt_ref[0], mine, ((0,), (0,)))
    for f in range(6):
        start, size = STARTS[f], SIZES[f]
        theirs = back_ref[0, 16 + 8 * f : 24 + 8 * f, :].astype(BF16).astype(F32)
        other = exact_dot(arrived[f][0, size : size + 8, :], theirs, ((0,), (0,)))
        if size > CASES:
            more = exact_dot(arrived[f][0, size + 8 : size + 16, :], theirs, ((0,), (0,)))
            other = jnp.concatenate([other, more[: size - CASES]], axis=0)
        resid = (gap_ref[0, start : start + size, :] - own[start : start + size]) - (
            arrived[f][0, :size, :] - other
        )
        p_ref[0, start : start + size, :] = resid - back_ref[0, f : f + 1, :]
    back = apply_to(p_ref[0], o_ref, ot_ref, flux_ref, first_ref, second_ref)
    for f in range(6):
        faces[f][0] = back(STARTS[f], SIZES[f])


VECTOR = (SPECIES, M, CASES)
FACES = [(SPECIES, size, CASES) for size in SIZES]
SCRATCH = [pltpu.VMEM((M, CASES), BF16), pltpu.VMEM((M, 2 * CASES), BF16)]


def start(gap, rt, back, o, ot, flux, arrived):
    return pl.pallas_call(
        start_kernel,
        grid=(SPECIES,),
        in_specs=[
            per_species(M, CASES),
            per_species(8, M),
            even(64, CASES),
            whole(M, M),
            whole(M, M),
            per_species(M, M),
        ]
        + [per_species(SIZES[f] + TAILS[f], CASES) for f in range(6)],
        out_specs=[per_species(M, CASES)] + [per_species(s, CASES) for s in SIZES],
        out_shape=[out(VECTOR)] + [out(shape) for shape in FACES],
        scratch_shapes=SCRATCH,
        compiler_params=params(),
        cost_estimate=cost(4e9, 20e6),
        name="start",
    )(gap, rt, back, o, ot, flux, *arrived)


def weights(info_ref):
    col, lay = info_ref[0], info_ref[1]
    xpos, ypos = col // YCOLS, col % YCOLS
    flags = [
        xpos > 0,
        xpos < NCOL // YCOLS - 1,
        ypos > 0,
        ypos < YCOLS - 1,
        lay > 0,
        lay < NLAY - 1,
    ]
    return [jnp.where(flag, 0.5, 1.0).astype(F32) for flag in flags]


def dots_kernel(same, info_ref, *refs):
    count = 1 if same else 2
    p_ref = refs[0]
    w_ref = refs[count - 1]
    faces = refs[count : count + 6]
    arrived = refs[count + 6 : count + 12]
    q_ref, msg_ref = refs[count + 12 :]
    weight = weights(info_ref)
    top = jnp.zeros((1, CASES), F32)
    for f in range(6):
        q = faces[f][0] - arrived[f][0]
        q_ref[0, STARTS[f] : STARTS[f] + SIZES[f], :] = q
        top = jnp.maximum(top, jnp.max(jnp.abs(q), axis=0, keepdims=True))
    top = jnp.where(top > 0.0, top, 1e-30)
    head, pq, qq, wq, ww = [jnp.zeros((1, CASES), F32) for _ in range(5)]

    def total(value):
        return jnp.sum(value, axis=0, keepdims=True)

    for f in range(6):
        here = slice(STARTS[f], STARTS[f] + SIZES[f])
        q = q_ref[0, here, :]
        p = p_ref[0, here, :]
        unit = q / top
        head = head + total(q)
        pq = pq + weight[f] * total(p * q)
        qq = qq + weight[f] * total(unit * unit)
        if same:
            ww = ww + weight[f] * total(p * p)
        else:
            w = w_ref[0, here, :]
            wq = wq + weight[f] * total(w * q)
            ww = ww + weight[f] * total(w * w)
    if same:
        wq = pq
    zero = jnp.zeros((1, CASES), F32)
    rows = (head, pq, qq, wq, ww, top, zero, zero)
    for r in range(8):
        msg_ref[0, r : r + 1, :] = rows[r]
        msg_ref[1, r : r + 1, :] = rows[r]


def dots(info, vectors, faces, arrived):
    same = len(vectors) == 1
    return pl.pallas_call(
        functools.partial(dots_kernel, same),
        grid=(SPECIES,),
        in_specs=[SMEM]
        + [per_species(M, CASES)] * len(vectors)
        + [per_species(s, CASES) for s in SIZES] * 2,
        out_specs=[per_species(M, CASES), pair(8, CASES)],
        out_shape=[out(VECTOR), out((8, 8, CASES))],
        compiler_params=params(),
        cost_estimate=cost(1e7, 10e6),
        name="dots",
    )(info, *vectors, *faces, *arrived)


def step_kernel(same, last, info_ref, back_ref, o_ref, ot_ref, flux_ref, *refs):
    count = 1 if same else 2
    p_ref = refs[0]
    w_ref = refs[count - 1]
    q_ref = refs[count]
    outs = refs[count + 1 : -2]
    first_ref, second_ref = refs[-2:]
    alpha = back_ref[0, 6:7, :]
    beta = back_ref[0, 7:8, :]
    weight = weights(info_ref)
    pnew_ref = outs[0]
    ww = jnp.zeros((1, CASES), F32)
    for f in range(6):
        here = slice(STARTS[f], STARTS[f] + SIZES[f])
        w = w_ref[0, here, :] - alpha * (q_ref[0, here, :] - back_ref[0, f : f + 1, :])
        if last:
            ww = ww + weight[f] * jnp.sum(w * w, axis=0, keepdims=True)
        else:
            outs[1][0, here, :] = w
        pnew_ref[0, here, :] = w + beta * p_ref[0, here, :]
    back = apply_to(pnew_ref[0], o_ref, ot_ref, flux_ref, first_ref, second_ref)
    if not last:
        for f in range(6):
            outs[2 + f][0] = back(STARTS[f], SIZES[f])
        return
    pq = jnp.zeros((1, CASES), F32)
    for i in range(0, M, CHUNK):
        g = back(i, CHUNK)
        pq = pq + jnp.sum(pnew_ref[0, i : i + CHUNK, :] * g, axis=0, keepdims=True)
    k = pl.program_id(0)
    msg_ref = outs[1]
    row = lax.broadcasted_iota(jnp.int32, (NLAY, 8, CASES), 1)
    held = msg_ref[...]
    held = jnp.where(row == k, pq[None], held)
    held = jnp.where(row == k + SPECIES, ww[None], held)
    msg_ref[...] = held


def step(info, back, o, ot, flux, vectors, q, last):
    same = len(vectors) == 1
    out_specs = [per_species(M, CASES)]
    out_shape = [out(VECTOR)]
    if last:
        out_specs += [whole(NLAY, 8, CASES)]
        out_shape += [out((NLAY, 8, CASES))]
    else:
        out_specs += [per_species(M, CASES)] + [per_species(s, CASES) for s in SIZES]
        out_shape += [out(VECTOR)] + [out(shape) for shape in FACES]
    return pl.pallas_call(
        functools.partial(step_kernel, same, last),
        grid=(SPECIES,),
        in_specs=[SMEM, even(8, CASES), whole(M, M), whole(M, M), per_species(M, M)]
        + [per_species(M, CASES)] * (len(vectors) + 1),
        out_specs=out_specs,
        out_shape=out_shape,
        scratch_shapes=SCRATCH,
        compiler_params=params(),
        cost_estimate=cost(4e9, 20e6),
        name="step",
    )(info, back, o, ot, flux, *vectors, q)


def finish_kernel(first_ref, back0_ref, back1_ref, sums_ref, p0_ref, p1_ref, p2_ref, out_ref):
    k = pl.program_id(0)
    sums = jnp.sum(sums_ref[...], axis=0)
    row = lax.broadcasted_iota(jnp.int32, (8, CASES), 0)
    pq = jnp.sum(jnp.where(row == k, sums, 0.0), axis=0, keepdims=True)
    ww = jnp.sum(jnp.where(row == k + SPECIES, sums, 0.0), axis=0, keepdims=True)
    alpha0 = back0_ref[0, 6:7, :]
    alpha1 = back1_ref[0, 6:7, :]
    alpha2 = ww / pq
    for f in range(6):
        here = slice(STARTS[f], STARTS[f] + SIZES[f])
        value = first_ref[0, 8 + f : 9 + f, :] + alpha0 * p0_ref[0, here, :]
        value = value + alpha1 * p1_ref[0, here, :]
        out_ref[0, here, :] = value + alpha2 * p2_ref[0, here, :]


def finish(first, back0, back1, sums, p0, p1, p2):
    return pl.pallas_call(
        finish_kernel,
        grid=(SPECIES,),
        in_specs=[even(64, CASES), even(8, CASES), even(8, CASES), whole(NCOL, 8, CASES)]
        + [per_species(M, CASES)] * 3,
        out_specs=per_species(M, CASES),
        out_shape=out(VECTOR),
        compiler_params=params(),
        cost_estimate=cost(1e7, 8e6),
        name="finish",
    )(first, back0, back1, sums, p0, p1, p2)


def exchange(blocks):
    def moved(value, axis, pairs):
        return lax.ppermute(value, axis, pairs)

    def along_x(step):
        return [(c, c + step) for c in range(NCOL) if 0 <= c + step < NCOL]

    def along_y(step):
        return [(c, c + step) for c in range(NCOL) if 0 <= c % YCOLS + step < YCOLS]

    def along_z(step):
        return [(l, l + step) for l in range(NLAY) if 0 <= l + step < NLAY]

    return [
        moved(blocks[1], "col", along_x(YCOLS)),
        moved(blocks[0], "col", along_x(-YCOLS)),
        moved(blocks[3], "col", along_y(1)),
        moved(blocks[2], "col", along_y(-1)),
        moved(blocks[5], "lay", along_z(1)),
        moved(blocks[4], "lay", along_z(-1)),
    ]


def swap(value, axis):
    return lax.all_to_all(value, axis, 0, 0, tiled=True)


def to_columns(value):
    return swap(jnp.broadcast_to(value[None], (NCOL,) + value.shape), "col")


def shards(flux_operator, dof_order, local_gap, rigid_load):
    flux = flux_operator[0, 0]
    order = dof_order[0, 0]
    gap = local_gap[0, 0]
    load = rigid_load[0, 0]
    info = jnp.stack([lax.axis_index("col"), lax.axis_index("lay")]).astype(jnp.int32)
    inverse = jnp.asarray(coarse_inverse())

    o, ot, rt, message, *faces = prep(order, flux, gap, load)
    arrived = exchange(faces)
    got = jnp.transpose(swap(message, "lay"), (1, 0, 2))
    back_first = swap(solve0(info, inverse, to_columns(got)), "lay")
    p0, *faces = start(gap, rt, back_first, o, ot, flux, arrived)

    q, message = dots(info, [p0], faces, exchange(faces))
    gathered = swap(mid(swap(message, "lay")), "col")
    back0 = swap(solve(info, inverse, gathered), "lay")
    p1, w1, *faces = step(info, back0, o, ot, flux, [p0], q, False)

    q, message = dots(info, [p1, w1], faces, exchange(faces))
    gathered = swap(mid(swap(message, "lay")), "col")
    back1 = swap(solve(info, inverse, gathered), "lay")
    p2, message = step(info, back1, o, ot, flux, [p1, w1], q, True)

    sums = to_columns(jnp.sum(swap(message, "lay"), axis=0))
    return finish(back_first, back0, back1, sums, p0, p1, p2)[None, None]


def solution(mesh):
    return jax.shard_map(
        shards,
        mesh=mesh,
        in_specs=(
            P("col", "lay", None, None, None),
            P("col", "lay", None),
            P("col", "lay", None, None, None),
            P("col", "lay", None, None),
        ),
        out_specs=P("col", "lay", None, None, None),
        check_vma=False,
    )
```

```python
import functools

import jax
import jax.numpy as jnp
import numpy as np
from jax import lax
from jax.experimental import pallas as pl
from jax.experimental.pallas import tpu as pltpu
from jax.sharding import PartitionSpec as P

SIDE = 192
TOP = 128
YCOLS = 4
SPECIES = 4
CASES = 128
M = 1024
NCOL = 32
NLAY = 8
COUNT = NCOL * NLAY
SIZES = (SIDE, SIDE, SIDE, SIDE, TOP, TOP)
STARTS = (0, 192, 384, 576, 768, 896)
TAILS = (16, 16, 16, 16, 8, 8)
CHUNK = 256
HALF = CASES // 2
F32 = jnp.float32
BF16 = jnp.bfloat16
VMEM_LIMIT = 40 * 1024 * 1024


def coarse_inverse():
    index = np.arange(COUNT)
    zpos, cpos = index % NLAY, index // NLAY
    ypos, xpos = cpos % YCOLS, cpos // YCOLS
    dx = np.abs(xpos[:, None] - xpos[None, :])
    dy = np.abs(ypos[:, None] - ypos[None, :])
    dz = np.abs(zpos[:, None] - zpos[None, :])
    lateral = (dx + dy == 1) & (dz == 0)
    upward = (dx + dy == 0) & (dz == 1)
    matrix = M * np.eye(COUNT) - SIDE * lateral - TOP * upward
    return np.linalg.inv(matrix).astype(np.float32)


def params():
    return pltpu.CompilerParams(
        dimension_semantics=("arbitrary",), vmem_limit_bytes=VMEM_LIMIT
    )


def cost(flops, nbytes):
    return pl.CostEstimate(flops=int(flops), bytes_accessed=int(nbytes), transcendentals=0)


SMEM = pl.BlockSpec(memory_space=pltpu.SMEM)


def per_species(*shape):
    zeros = (0,) * len(shape)
    return pl.BlockSpec((1,) + shape, lambda k: (jnp.minimum(k, SPECIES - 1),) + zeros)


def whole(*shape):
    zeros = (0,) * len(shape)
    return pl.BlockSpec(shape, lambda k: zeros)


def pair(*shape):
    zeros = (0,) * len(shape)
    return pl.BlockSpec((2,) + shape, lambda k: (jnp.minimum(k, SPECIES - 1),) + zeros)


def out(shape, dtype=F32):
    return jax.ShapeDtypeStruct(shape, dtype)


def exact_dot(a, b, dims):
    return lax.dot_general(
        a, b, (dims, ((), ())), precision=lax.Precision.HIGHEST, preferred_element_type=F32
    )


def split3(value):
    first = value.astype(BF16).astype(F32)
    rest = value - first
    second = rest.astype(BF16).astype(F32)
    return [first, second, rest - second]


def fill_gather(col_ref, o_ref):
    lanes = lax.broadcasted_iota(jnp.int32, (CHUNK, M), 1)
    for i in range(0, M, CHUNK):
        hit = col_ref[i : i + CHUNK, :] == lanes
        o_ref[i : i + CHUNK, :] = jnp.where(hit, 1.0, 0.0).astype(BF16)


def fill_scatter(row_ref, ot_ref):
    row = row_ref[...]
    index = lax.broadcasted_iota(jnp.int32, (CHUNK, M), 0)
    for i in range(0, M, CHUNK):
        hit = row == index + i
        ot_ref[i : i + CHUNK, :] = jnp.where(hit, 1.0, 0.0).astype(BF16)


def prep_kernel(row_ref, col_ref, flux_ref, gap_ref, load_ref, *refs):
    rt_ref, msg_ref = refs[:2]
    face_refs = refs[2:8]
    parts_ref, o_ref = refs[8:]
    k = pl.program_id(0)
    row = row_ref[...]

    face = lax.broadcasted_iota(jnp.int32, (16, M), 0)
    low = jnp.where(face <= 4, SIDE * face, jnp.where(face == 5, STARTS[5], M))
    high = jnp.where(face <= 3, SIDE * (face + 1), jnp.where(face == 4, STARTS[5], M))
    member = jnp.where((row >= low) & (row < high), 1.0, 0.0).astype(BF16)
    sums = jnp.dot(member, flux_ref[0], preferred_element_type=F32)
    for i, part in enumerate(split3(sums)):
        parts_ref[k, 16 * i : 16 * i + 16, :] = part.astype(BF16)
    rows = [
        jnp.sum(gap_ref[0, STARTS[f] : STARTS[f] + SIZES[f], :], axis=0, keepdims=True)
        for f in range(6)
    ]
    rows.append(load_ref[0])
    held = jnp.concatenate(rows + [jnp.zeros((1, CASES), F32)], axis=0)
    msg_ref[2 * k] = held
    msg_ref[2 * k + 1] = held
    for f in range(6):
        face_refs[f][k, : SIZES[f], :] = gap_ref[0, STARTS[f] : STARTS[f] + SIZES[f], :]

    @pl.when(k == SPECIES - 1)
    def _():
        fill_gather(col_ref, o_ref)
        parts = parts_ref[...].reshape(SPECIES * 48, M)
        moved = jnp.dot(parts, o_ref[...], preferred_element_type=F32)
        lane = lax.broadcasted_iota(jnp.int32, (8, M), 1)
        slot = lax.broadcasted_iota(jnp.int32, (8, CASES), 1)
        peer = lax.broadcasted_iota(jnp.int32, (8, CASES), 0)
        for s in range(SPECIES):
            base = 48 * s
            rt = moved[base : base + 8] + moved[base + 16 : base + 24]
            rt = rt + moved[base + 32 : base + 40]
            rt_ref[s] = rt
            table = jnp.zeros((8, CASES), F32)
            for f in range(6):
                inside = (lane >= STARTS[f]) & (lane < STARTS[f] + SIZES[f])
                total = jnp.sum(jnp.where(inside, rt, 0.0), axis=1, keepdims=True)
                here = (slot == 6 * f + peer) & (peer < 6)
                table = table + jnp.where(here, total, 0.0)
            table = jnp.sum(table, axis=0, keepdims=True)
            msg_ref[2 * s, 7:8, :] = table
            msg_ref[2 * s + 1, 7:8, :] = table
            for f in range(6):
                size = SIZES[f]
                turned = rt if STARTS[f] == 0 else pltpu.roll(rt, M - STARTS[f], 1)
                face_refs[f][s, size : size + 8, :] = turned[:, :CASES]
                if size > CASES:
                    face_refs[f][s, size + 8 : size + 16, :] = turned[:, CASES : 2 * CASES]


def prep(row, column, flux, gap, load):
    faces = [(SPECIES, SIZES[f] + TAILS[f], CASES) for f in range(6)]
    return pl.pallas_call(
        prep_kernel,
        grid=(SPECIES,),
        in_specs=[
            whole(1, M),
            whole(M, 1),
            per_species(M, M),
            per_species(M, CASES),
            per_species(1, CASES),
        ],
        out_specs=[whole(SPECIES, 8, M), whole(8, 8, CASES)]
        + [whole(*shape) for shape in faces],
        out_shape=[
            out((SPECIES, 8, M)),
            out((8, 8, CASES)),
        ]
        + [out(shape) for shape in faces],
        scratch_shapes=[pltpu.VMEM((SPECIES, 48, M), BF16), pltpu.VMEM((M, M), BF16)],
        compiler_params=params(),
        cost_estimate=cost(1e9, 20e6),
        name="prep",
    )(row, column, flux, gap, load.reshape(SPECIES, 1, CASES))


def shifted(value, f):
    row = lax.broadcasted_iota(jnp.int32, value.shape, 0)
    zpos = row % NLAY
    ypos = (row // NLAY) % YCOLS
    xpos = row // (NLAY * YCOLS)
    step, ok = (
        (NLAY * YCOLS, xpos > 0),
        (-NLAY * YCOLS, xpos < NCOL // YCOLS - 1),
        (NLAY, ypos > 0),
        (-NLAY, ypos < YCOLS - 1),
        (1, zpos > 0),
        (-1, zpos < NLAY - 1),
    )[f]
    return jnp.where(ok, pltpu.roll(value, step % COUNT, 0), 0.0)


def own_half(value, lay):
    return jnp.where(lay % 2 == 0, value, pltpu.roll(value, HALF, value.ndim - 1))


def packed(first, second):
    lane = lax.broadcasted_iota(jnp.int32, first.shape, first.ndim - 1)
    return jnp.where(lane < HALF, first, pltpu.roll(second, HALF, second.ndim - 1))


def mid0_kernel(info_ref, got_ref, out_ref):
    lay = info_ref[1]

    def rows(r):
        return jnp.concatenate([got_ref[l, r : r + 1, :] for l in range(NLAY)], axis=0)

    halves = [own_half(rows(r), lay) for r in range(7)] + [rows(7)]
    tiles = [packed(halves[r], halves[r + 4]) for r in range(4)]
    for c in range(NCOL):
        for r in range(4):
            out_ref[c, r] = tiles[r]


def mid0(info, got):
    return pl.pallas_call(
        mid0_kernel,
        in_specs=[SMEM, pl.BlockSpec(memory_space=pltpu.VMEM)],
        out_specs=pl.BlockSpec(memory_space=pltpu.VMEM),
        out_shape=out((NCOL, 4, 8, CASES)),
        cost_estimate=cost(1e5, 6e5),
        name="pack_start",
    )(info, got)


def solve0_kernel(info_ref, inv_ref, gathered_ref, out_ref, vals_ref):
    col = info_ref[0]

    def rows(r):
        value = gathered_ref[:, r % 4].reshape(COUNT, CASES)
        return value if r < 4 else pltpu.roll(value, HALF, 1)

    inv = inv_ref[...]
    y0 = exact_dot(inv, rows(6), ((1,), (0,)))
    vals = [y0 - shifted(y0, f) for f in range(6)]
    rounded = [v.astype(BF16).astype(F32) for v in vals]
    table = rows(7)
    tau = []
    for f in range(6):
        total = rows(f)
        for g in range(6):
            total = total - table[:, 6 * f + g : 6 * f + g + 1] * rounded[g]
        tau.append(total)
    h = jnp.zeros((COUNT, CASES), F32)
    for f in range(6):
        h = h + (tau[f] - shifted(tau[f ^ 1], f))
    y1 = exact_dot(inv, h, ((1,), (0,)))
    here = pl.ds(pl.multiple_of(col * NLAY, NLAY), NLAY)
    zero = jnp.zeros((NLAY, CASES), F32)
    for f in range(6):
        vals_ref[0] = y1 - shifted(y1, f)
        out_ref[:, f, :] = vals_ref[0, here, :]
    for f in range(6):
        vals_ref[f] = vals[f]
    for g in range(6):
        out_ref[:, 8 + g, :] = vals_ref[g, here, :]
    for f in range(4):
        away = jnp.clip(col + (-YCOLS, YCOLS, -1, 1)[f], 0, NCOL - 1)
        there = pl.ds(pl.multiple_of(away * NLAY, NLAY), NLAY)
        for g in range(6):
            out_ref[:, 16 + 8 * f + g, :] = vals_ref[g, there, :]
    for f in (4, 5):
        for g in range(6):
            out_ref[:, 16 + 8 * f + g, :] = pltpu.roll(
                vals_ref[g, here, :], (1, NLAY - 1)[f - 4], 0
            )
    for group in range(8):
        out_ref[:, 8 * group + 6, :] = zero
        out_ref[:, 8 * group + 7, :] = zero


def solve0(info, inverse, gathered):
    return pl.pallas_call(
        solve0_kernel,
        in_specs=[SMEM, pl.BlockSpec(memory_space=pltpu.VMEM), pl.BlockSpec(memory_space=pltpu.VMEM)],
        out_specs=pl.BlockSpec(memory_space=pltpu.VMEM),
        out_shape=out((8, 64, CASES)),
        scratch_shapes=[pltpu.VMEM((6, COUNT, CASES), F32)],
        compiler_params=pltpu.CompilerParams(vmem_limit_bytes=VMEM_LIMIT),
        cost_estimate=cost(1e8, 2e6),
        name="solve_start",
    )(info, inverse, gathered)


def mid_kernel(info_ref, got_ref, out_ref):
    lay = info_ref[1]
    total = got_ref[0]
    top = got_ref[0, 5:6, :]
    for l in range(1, NLAY):
        total = total + got_ref[l]
        top = jnp.maximum(top, got_ref[l, 5:6, :])
    qq = jnp.zeros((1, CASES), F32)
    for l in range(NLAY):
        part = got_ref[l, 5:6, :] / top
        qq = qq + got_ref[l, 2:3, :] * (part * part)
    heads = [got_ref[l, 0:1, :] for l in range(NLAY)]
    zero = jnp.zeros((1, CASES), F32)
    first = jnp.concatenate(heads[:4] + [total[1:2], total[3:4], top, zero], axis=0)
    second = jnp.concatenate(heads[4:] + [qq, total[4:5], top, zero], axis=0)
    tile = packed(own_half(first, lay), own_half(second, lay))
    for c in range(NCOL):
        out_ref[c] = tile


def mid(info, got):
    return pl.pallas_call(
        mid_kernel,
        in_specs=[SMEM, pl.BlockSpec(memory_space=pltpu.VMEM)],
        out_specs=pl.BlockSpec(memory_space=pltpu.VMEM),
        out_shape=out((NCOL, 8, CASES)),
        cost_estimate=cost(1e5, 3e5),
        name="combine_layers",
    )(info, got)


def solve_kernel(info_ref, inv_ref, gathered_ref, out_ref, y_ref):
    col = info_ref[0]
    tiles = gathered_ref[...].reshape(COUNT, CASES)
    upper = pltpu.roll(tiles, HALF, 1)
    row = lax.broadcasted_iota(jnp.int32, (COUNT, CASES), 0) % 8
    tops = jnp.where(row == 6, tiles, 0.0)
    top = jnp.max(tops, axis=0, keepdims=True)
    part = pltpu.roll(tops, COUNT - 2, 0) / top
    qq = jnp.sum(jnp.where(row == 4, upper * (part * part), 0.0), axis=0, keepdims=True)
    pq = jnp.sum(jnp.where(row == 4, tiles, 0.0), axis=0, keepdims=True)
    wq = jnp.sum(jnp.where(row == 5, tiles, 0.0), axis=0, keepdims=True)
    energy = jnp.sum(jnp.where(row == 5, upper, 0.0), axis=0, keepdims=True)
    h = jnp.where(row < 4, tiles, pltpu.roll(upper, 4, 0)) / top
    y = exact_dot(inv_ref[...], h, ((1,), (0,)))
    hy = jnp.sum(h * y, axis=0, keepdims=True)
    alpha = energy / pq
    scaled = alpha * top
    new = energy - 2.0 * (alpha * wq) + (scaled * scaled) * (qq - hy)
    beta = new / energy
    y = y * top
    here = pl.ds(pl.multiple_of(col * NLAY, NLAY), NLAY)
    for f in range(6):
        y_ref[...] = y - shifted(y, f)
        out_ref[:, f, :] = y_ref[here, :]
    out_ref[:, 6, :] = jnp.broadcast_to(alpha, (NLAY, CASES))
    out_ref[:, 7, :] = jnp.broadcast_to(beta, (NLAY, CASES))


def solve(info, inverse, gathered):
    return pl.pallas_call(
        solve_kernel,
        in_specs=[SMEM, pl.BlockSpec(memory_space=pltpu.VMEM), pl.BlockSpec(memory_space=pltpu.VMEM)],
        out_specs=pl.BlockSpec(memory_space=pltpu.VMEM),
        out_shape=out((8, 8, CASES)),
        scratch_shapes=[pltpu.VMEM((COUNT, CASES), F32)],
        cost_estimate=cost(1e8, 1e6),
        name="solve_step",
    )(info, inverse, gathered)


ANY = pl.BlockSpec(memory_space=pl.ANY)
SCRATCH = [
    pltpu.VMEM((M, SPECIES * CASES), BF16),
    pltpu.VMEM((M, 2 * SPECIES * CASES), BF16),
    pltpu.VMEM((M, M), BF16),
    pltpu.VMEM((M, M), BF16),
    pltpu.VMEM((SPECIES, M, M), BF16),
    pltpu.SemaphoreType.DMA((SPECIES,)),
]


def fetches(flux_ref, scratch):
    flux_vmem, sems = scratch[4:]
    return [
        pltpu.make_async_copy(flux_ref.at[k], flux_vmem.at[k], sems.at[k])
        for k in range(SPECIES)
    ]


def store_direction(k, value, scratch):
    for s in range(SPECIES):

        @pl.when(k == s)
        def _():
            scratch[0][:, s * CASES : (s + 1) * CASES] = value.astype(BF16)


def apply_all(row_ref, col_ref, copies, scratch):
    x_ref, both_ref, o_vmem, ot_vmem, flux_vmem, _ = scratch
    wide = SPECIES * CASES
    fill_gather(col_ref, o_vmem)
    x_ref[...] = jnp.dot(o_vmem[...], x_ref[...], preferred_element_type=F32).astype(BF16)
    fill_scatter(row_ref, ot_vmem)
    for k in range(SPECIES):
        here = slice(k * CASES, (k + 1) * CASES)
        copies[k].wait()
        image = jnp.dot(flux_vmem[k], x_ref[:, here], preferred_element_type=F32)
        high = image.astype(BF16)
        both_ref[:, here] = high
        both_ref[:, wide + k * CASES : wide + (k + 1) * CASES] = (
            image - high.astype(F32)
        ).astype(BF16)


def moved_back(scratch, start, size):
    both_ref, ot_vmem = scratch[1], scratch[3]
    wide = SPECIES * CASES
    both = jnp.dot(ot_vmem[start : start + size, :], both_ref[...], preferred_element_type=F32)
    return both[:, :wide] + both[:, wide:]


def store_faces(scratch, faces):
    for first in (0, 2, 4):
        begin = STARTS[first]
        image = moved_back(scratch, begin, SIZES[first] + SIZES[first + 1])
        for f in (first, first + 1):
            offset = STARTS[f] - begin
            for k in range(SPECIES):
                faces[f][k] = image[offset : offset + SIZES[f], k * CASES : (k + 1) * CASES]


def merged(ref):
    lane = lax.broadcasted_iota(jnp.int32, ref.shape[1:], 1)
    return jnp.where(lane < HALF, ref[0], pltpu.roll(ref[1], HALF, 1))


def turned_dot(rt, values):
    left = jnp.concatenate(split3(rt), axis=0).astype(BF16)
    right = jnp.concatenate([values] * 3, axis=0).astype(BF16)
    return lax.dot_general(left, right, (((0,), (0,)), ((), ())), preferred_element_type=F32)


def start_kernel(gap_ref, rt_ref, back_ref, row_ref, col_ref, flux_ref, *refs):
    arrived = refs[:6]
    p_ref = refs[6]
    faces = refs[7:13]
    scratch = refs[13:]
    k = pl.program_id(0)
    copies = fetches(flux_ref, scratch)

    @pl.when(k == 0)
    def _():
        for copy in copies:
            copy.start()

    @pl.when(k < SPECIES)
    def _():
        table = merged(back_ref)
        own = turned_dot(rt_ref[0], table[8:16])
        for f in range(6):
            start, size = STARTS[f], SIZES[f]
            theirs = table[16 + 8 * f : 24 + 8 * f]
            other = turned_dot(arrived[f][0, size : size + 8, :], theirs)
            if size > CASES:
                more = turned_dot(arrived[f][0, size + 8 : size + 16, :], theirs)
                other = jnp.concatenate([other, more[: size - CASES]], axis=0)
            resid = (gap_ref[0, start : start + size, :] - own[start : start + size]) - (
                arrived[f][0, :size, :] - other
            )
            p_ref[0, start : start + size, :] = resid - table[f : f + 1, :]
        store_direction(k, p_ref[0], scratch)

    @pl.when(k == SPECIES)
    def _():
        apply_all(row_ref, col_ref, copies, scratch)
        store_faces(scratch, faces)


VECTOR = (SPECIES, M, CASES)
FACES = [(SPECIES, size, CASES) for size in SIZES]


def start(gap, rt, back, row, column, flux, arrived):
    return pl.pallas_call(
        start_kernel,
        grid=(SPECIES + 1,),
        in_specs=[
            per_species(M, CASES),
            per_species(8, M),
            pair(64, CASES),
            whole(1, M),
            whole(M, 1),
            ANY,
        ]
        + [per_species(SIZES[f] + TAILS[f], CASES) for f in range(6)],
        out_specs=[per_species(M, CASES)] + [whole(*shape) for shape in FACES],
        out_shape=[out(VECTOR)] + [out(shape) for shape in FACES],
        scratch_shapes=SCRATCH,
        compiler_params=params(),
        cost_estimate=cost(4e9, 20e6),
        name="start",
    )(gap, rt, back, row, column, flux, *arrived)


def weights(info_ref):
    col, lay = info_ref[0], info_ref[1]
    xpos, ypos = col // YCOLS, col % YCOLS
    flags = [
        xpos > 0,
        xpos < NCOL // YCOLS - 1,
        ypos > 0,
        ypos < YCOLS - 1,
        lay > 0,
        lay < NLAY - 1,
    ]
    return [jnp.where(flag, 0.5, 1.0).astype(F32) for flag in flags]


def dots_kernel(same, info_ref, *refs):
    count = 1 if same else 2
    p_ref = refs[0]
    w_ref = refs[count - 1]
    faces = refs[count : count + 6]
    arrived = refs[count + 6 : count + 12]
    q_ref, msg_ref = refs[count + 12 :]
    weight = weights(info_ref)
    top = jnp.zeros((1, CASES), F32)
    for f in range(6):
        q = faces[f][0] - arrived[f][0]
        q_ref[0, STARTS[f] : STARTS[f] + SIZES[f], :] = q
        top = jnp.maximum(top, jnp.max(jnp.abs(q), axis=0, keepdims=True))
    top = jnp.where(top > 0.0, top, 1e-30)
    head, pq, qq, wq, ww = [jnp.zeros((1, CASES), F32) for _ in range(5)]

    def total(value):
        return jnp.sum(value, axis=0, keepdims=True)

    for f in range(6):
        here = slice(STARTS[f], STARTS[f] + SIZES[f])
        q = q_ref[0, here, :]
        p = p_ref[0, here, :]
        unit = q / top
        head = head + total(q)
        pq = pq + weight[f] * total(p * q)
        qq = qq + weight[f] * total(unit * unit)
        if same:
            ww = ww + weight[f] * total(p * p)
        else:
            w = w_ref[0, here, :]
            wq = wq + weight[f] * total(w * q)
            ww = ww + weight[f] * total(w * w)
    if same:
        wq = pq
    zero = jnp.zeros((1, CASES), F32)
    rows = (head, pq, qq, wq, ww, top, zero, zero)
    for r in range(8):
        msg_ref[0, r : r + 1, :] = rows[r]
        msg_ref[1, r : r + 1, :] = rows[r]


def dots(info, vectors, faces, arrived):
    same = len(vectors) == 1
    return pl.pallas_call(
        functools.partial(dots_kernel, same),
        grid=(SPECIES,),
        in_specs=[SMEM]
        + [per_species(M, CASES)] * len(vectors)
        + [per_species(s, CASES) for s in SIZES] * 2,
        out_specs=[per_species(M, CASES), pair(8, CASES)],
        out_shape=[out(VECTOR), out((8, 8, CASES))],
        compiler_params=params(),
        cost_estimate=cost(1e7, 10e6),
        name="dots",
    )(info, *vectors, *faces, *arrived)


def step_kernel(same, last, info_ref, back_ref, row_ref, col_ref, flux_ref, *refs):
    count = 1 if same else 2
    p_ref = refs[0]
    w_ref = refs[count - 1]
    q_ref = refs[count]
    outs = refs[count + 1 : -len(SCRATCH) - 1]
    scratch = refs[-len(SCRATCH) - 1 : -1]
    held_ref = refs[-1]
    k = pl.program_id(0)
    copies = fetches(flux_ref, scratch)

    @pl.when(k == 0)
    def _():
        for copy in copies:
            copy.start()

    @pl.when(k < SPECIES)
    def _():
        table = merged(back_ref)
        alpha, beta = table[6:7], table[7:8]
        weight = weights(info_ref)
        ww = jnp.zeros((1, CASES), F32)
        for f in range(6):
            here = slice(STARTS[f], STARTS[f] + SIZES[f])
            w = w_ref[0, here, :] - alpha * (q_ref[0, here, :] - table[f : f + 1, :])
            if last:
                ww = ww + weight[f] * jnp.sum(w * w, axis=0, keepdims=True)
            else:
                outs[1][0, here, :] = w
            outs[0][0, here, :] = w + beta * p_ref[0, here, :]
        store_direction(k, outs[0][0], scratch)
        if last:
            held_ref[k] = outs[0][0]
            row = lax.broadcasted_iota(jnp.int32, (NLAY, 8, CASES), 1)
            outs[1][...] = jnp.where(row == k + SPECIES, ww[None], outs[1][...])

    @pl.when(k == SPECIES)
    def _():
        apply_all(row_ref, col_ref, copies, scratch)
        if not last:
            store_faces(scratch, outs[2:])
            return
        sums = [jnp.zeros((1, CASES), F32) for _ in range(SPECIES)]
        for i in range(0, M, M // 2):
            image = moved_back(scratch, i, M // 2)
            for s in range(SPECIES):
                part = held_ref[s, i : i + M // 2] * image[:, s * CASES : (s + 1) * CASES]
                sums[s] = sums[s] + jnp.sum(part, axis=0, keepdims=True)
        for s in range(SPECIES):
            pq = sums[s]
            for l in range(NLAY):
                outs[1][l, s : s + 1, :] = pq


def step(info, back, row, column, flux, vectors, q, last):
    same = len(vectors) == 1
    out_specs = [per_species(M, CASES)]
    out_shape = [out(VECTOR)]
    if last:
        out_specs += [whole(NLAY, 8, CASES)]
        out_shape += [out((NLAY, 8, CASES))]
    else:
        out_specs += [per_species(M, CASES)] + [whole(*shape) for shape in FACES]
        out_shape += [out(VECTOR)] + [out(shape) for shape in FACES]
    held = pltpu.VMEM(VECTOR if last else (1, 8, CASES), F32)
    return pl.pallas_call(
        functools.partial(step_kernel, same, last),
        grid=(SPECIES + 1,),
        in_specs=[SMEM, pair(8, CASES), whole(1, M), whole(M, 1), ANY]
        + [per_species(M, CASES)] * (len(vectors) + 1),
        out_specs=out_specs,
        out_shape=out_shape,
        scratch_shapes=SCRATCH + [held],
        compiler_params=params(),
        cost_estimate=cost(4e9, 20e6),
        name="step",
    )(info, back, row, column, flux, *vectors, q)


def finish_kernel(first_ref, back0_ref, back1_ref, sums_ref, p0_ref, p1_ref, p2_ref, out_ref):
    k = pl.program_id(0)
    sums = jnp.sum(sums_ref[...], axis=0)
    row = lax.broadcasted_iota(jnp.int32, (8, CASES), 0)
    pq = jnp.sum(jnp.where(row == k, sums, 0.0), axis=0, keepdims=True)
    ww = jnp.sum(jnp.where(row == k + SPECIES, sums, 0.0), axis=0, keepdims=True)
    initial = merged(first_ref)
    alpha0 = merged(back0_ref)[6:7]
    alpha1 = merged(back1_ref)[6:7]
    alpha2 = ww / pq
    for f in range(6):
        here = slice(STARTS[f], STARTS[f] + SIZES[f])
        value = initial[8 + f : 9 + f] + alpha0 * p0_ref[0, here, :]
        value = value + alpha1 * p1_ref[0, here, :]
        out_ref[0, here, :] = value + alpha2 * p2_ref[0, here, :]


def finish(first, back0, back1, sums, p0, p1, p2):
    return pl.pallas_call(
        finish_kernel,
        grid=(SPECIES,),
        in_specs=[pair(64, CASES), pair(8, CASES), pair(8, CASES), whole(NCOL, 8, CASES)]
        + [per_species(M, CASES)] * 3,
        out_specs=per_species(M, CASES),
        out_shape=out(VECTOR),
        compiler_params=params(),
        cost_estimate=cost(1e7, 8e6),
        name="finish",
    )(first, back0, back1, sums, p0, p1, p2)


def exchange(blocks):
    def moved(value, axis, pairs):
        return lax.ppermute(value, axis, pairs)

    def along_x(step):
        return [(c, c + step) for c in range(NCOL) if 0 <= c + step < NCOL]

    def along_y(step):
        return [(c, c + step) for c in range(NCOL) if 0 <= c % YCOLS + step < YCOLS]

    def along_z(step):
        return [(l, l + step) for l in range(NLAY) if 0 <= l + step < NLAY]

    return [
        moved(blocks[1], "col", along_x(YCOLS)),
        moved(blocks[0], "col", along_x(-YCOLS)),
        moved(blocks[3], "col", along_y(1)),
        moved(blocks[2], "col", along_y(-1)),
        moved(blocks[5], "lay", along_z(1)),
        moved(blocks[4], "lay", along_z(-1)),
    ]


def swap(value, axis):
    return lax.all_to_all(value, axis, 0, 0, tiled=True)


def to_columns(value):
    return swap(jnp.broadcast_to(value[None], (NCOL,) + value.shape), "col")


def shards(flux_operator, dof_order, local_gap, rigid_load):
    flux = flux_operator[0, 0]
    order = dof_order[0, 0]
    gap = local_gap[0, 0]
    load = rigid_load[0, 0]
    info = jnp.stack([lax.axis_index("col"), lax.axis_index("lay")]).astype(jnp.int32)
    inverse = jnp.asarray(coarse_inverse())

    row, column = order.reshape(1, M), order.reshape(M, 1)
    rt, message, *faces = prep(row, column, flux, gap, load)
    arrived = exchange(faces)
    packed_start = mid0(info, swap(message, "lay"))
    back_first = swap(solve0(info, inverse, swap(packed_start, "col")), "lay")
    p0, *faces = start(gap, rt, back_first, row, column, flux, arrived)

    q, message = dots(info, [p0], faces, exchange(faces))
    gathered = swap(mid(info, swap(message, "lay")), "col")
    back0 = swap(solve(info, inverse, gathered), "lay")
    p1, w1, *faces = step(info, back0, row, column, flux, [p0], q, False)

    q, message = dots(info, [p1, w1], faces, exchange(faces))
    gathered = swap(mid(info, swap(message, "lay")), "col")
    back1 = swap(solve(info, inverse, gathered), "lay")
    p2, message = step(info, back1, row, column, flux, [p1, w1], q, True)

    sums = to_columns(jnp.sum(swap(message, "lay"), axis=0))
    return finish(back_first, back0, back1, sums, p0, p1, p2)[None, None]


def solution(mesh):
    return jax.shard_map(
        shards,
        mesh=mesh,
        in_specs=(
            P("col", "lay", None, None, None),
            P("col", "lay", None),
            P("col", "lay", None, None, None),
            P("col", "lay", None, None),
        ),
        out_specs=P("col", "lay", None, None, None),
        check_vma=False,
    )
```

```python
import functools

import jax
import jax.numpy as jnp
import numpy as np
from jax import lax
from jax.experimental import pallas as pl
from jax.experimental.pallas import tpu as pltpu
from jax.sharding import PartitionSpec as P

SIDE = 192
TOP = 128
YCOLS = 4
SPECIES = 4
CASES = 128
M = 1024
NCOL = 32
NLAY = 8
COUNT = NCOL * NLAY
SIZES = (SIDE, SIDE, SIDE, SIDE, TOP, TOP)
STARTS = (0, 192, 384, 576, 768, 896)
TAILS = (16, 16, 16, 16, 8, 8)
CHUNK = 256
HALF = CASES // 2
F32 = jnp.float32
BF16 = jnp.bfloat16
MIB = 1024 * 1024
VMEM_LIMIT = 40 * MIB


def coarse_inverse():
    index = np.arange(COUNT)
    zpos, cpos = index % NLAY, index // NLAY
    ypos, xpos = cpos % YCOLS, cpos // YCOLS
    dx = np.abs(xpos[:, None] - xpos[None, :])
    dy = np.abs(ypos[:, None] - ypos[None, :])
    dz = np.abs(zpos[:, None] - zpos[None, :])
    lateral = (dx + dy == 1) & (dz == 0)
    upward = (dx + dy == 0) & (dz == 1)
    matrix = M * np.eye(COUNT) - SIDE * lateral - TOP * upward
    return np.linalg.inv(matrix).astype(np.float32)


def params(limit=VMEM_LIMIT):
    return pltpu.CompilerParams(
        dimension_semantics=("arbitrary",), vmem_limit_bytes=limit
    )


def small(limit):
    return pltpu.CompilerParams(vmem_limit_bytes=limit * MIB)


def cost(flops, nbytes):
    return pl.CostEstimate(flops=int(flops), bytes_accessed=int(nbytes), transcendentals=0)


SMEM = pl.BlockSpec(memory_space=pltpu.SMEM)


def per_species(*shape):
    zeros = (0,) * len(shape)
    return pl.BlockSpec((1,) + shape, lambda k: (jnp.minimum(k, SPECIES - 1),) + zeros)


def whole(*shape):
    zeros = (0,) * len(shape)
    return pl.BlockSpec(shape, lambda k: zeros)


def pair(*shape):
    zeros = (0,) * len(shape)
    return pl.BlockSpec((2,) + shape, lambda k: (jnp.minimum(k, SPECIES - 1),) + zeros)


def out(shape, dtype=F32):
    return jax.ShapeDtypeStruct(shape, dtype)


def exact_dot(a, b, dims):
    return lax.dot_general(
        a, b, (dims, ((), ())), precision=lax.Precision.HIGHEST, preferred_element_type=F32
    )


def split3(value):
    first = value.astype(BF16).astype(F32)
    rest = value - first
    second = rest.astype(BF16).astype(F32)
    return [first, second, rest - second]


def fill_gather(col_ref, o_ref):
    lanes = lax.broadcasted_iota(jnp.int32, (CHUNK, M), 1)
    for i in range(0, M, CHUNK):
        hit = col_ref[i : i + CHUNK, :] == lanes
        o_ref[i : i + CHUNK, :] = jnp.where(hit, 1.0, 0.0).astype(BF16)


def fill_scatter(row_ref, ot_ref):
    row = row_ref[...]
    index = lax.broadcasted_iota(jnp.int32, (CHUNK, M), 0)
    for i in range(0, M, CHUNK):
        hit = row == index + i
        ot_ref[i : i + CHUNK, :] = jnp.where(hit, 1.0, 0.0).astype(BF16)


def prep_kernel(row_ref, col_ref, flux_ref, gap_ref, load_ref, *refs):
    rt_ref, msg_ref = refs[:2]
    face_refs = refs[2:8]
    parts_ref, o_ref = refs[8:]
    k = pl.program_id(0)
    row = row_ref[...]

    face = lax.broadcasted_iota(jnp.int32, (16, M), 0)
    low = jnp.where(face <= 4, SIDE * face, jnp.where(face == 5, STARTS[5], M))
    high = jnp.where(face <= 3, SIDE * (face + 1), jnp.where(face == 4, STARTS[5], M))
    member = jnp.where((row >= low) & (row < high), 1.0, 0.0).astype(BF16)
    sums = jnp.dot(member, flux_ref[0], preferred_element_type=F32)
    for i, part in enumerate(split3(sums)):
        parts_ref[k, 16 * i : 16 * i + 16, :] = part.astype(BF16)
    rows = [
        jnp.sum(gap_ref[0, STARTS[f] : STARTS[f] + SIZES[f], :], axis=0, keepdims=True)
        for f in range(6)
    ]
    rows.append(load_ref[0])
    held = jnp.concatenate(rows + [jnp.zeros((1, CASES), F32)], axis=0)
    msg_ref[2 * k] = held
    msg_ref[2 * k + 1] = held
    for f in range(6):
        face_refs[f][k, : SIZES[f], :] = gap_ref[0, STARTS[f] : STARTS[f] + SIZES[f], :]

    @pl.when(k == SPECIES - 1)
    def _():
        fill_gather(col_ref, o_ref)
        parts = parts_ref[...].reshape(SPECIES * 48, M)
        moved = jnp.dot(parts, o_ref[...], preferred_element_type=F32)
        lane = lax.broadcasted_iota(jnp.int32, (8, M), 1)
        slot = lax.broadcasted_iota(jnp.int32, (8, CASES), 1)
        peer = lax.broadcasted_iota(jnp.int32, (8, CASES), 0)
        for s in range(SPECIES):
            base = 48 * s
            rt = moved[base : base + 8] + moved[base + 16 : base + 24]
            rt = rt + moved[base + 32 : base + 40]
            rt_ref[s] = rt
            table = jnp.zeros((8, CASES), F32)
            for f in range(6):
                inside = (lane >= STARTS[f]) & (lane < STARTS[f] + SIZES[f])
                total = jnp.sum(jnp.where(inside, rt, 0.0), axis=1, keepdims=True)
                here = (slot == 6 * f + peer) & (peer < 6)
                table = table + jnp.where(here, total, 0.0)
            table = jnp.sum(table, axis=0, keepdims=True)
            msg_ref[2 * s, 7:8, :] = table
            msg_ref[2 * s + 1, 7:8, :] = table
            for f in range(6):
                size = SIZES[f]
                turned = rt if STARTS[f] == 0 else pltpu.roll(rt, M - STARTS[f], 1)
                face_refs[f][s, size : size + 8, :] = turned[:, :CASES]
                if size > CASES:
                    face_refs[f][s, size + 8 : size + 16, :] = turned[:, CASES : 2 * CASES]


def prep(row, column, flux, gap, load):
    faces = [(SPECIES, SIZES[f] + TAILS[f], CASES) for f in range(6)]
    return pl.pallas_call(
        prep_kernel,
        grid=(SPECIES,),
        in_specs=[
            whole(1, M),
            whole(M, 1),
            per_species(M, M),
            per_species(M, CASES),
            per_species(1, CASES),
        ],
        out_specs=[whole(SPECIES, 8, M), whole(8, 8, CASES)]
        + [whole(*shape) for shape in faces],
        out_shape=[
            out((SPECIES, 8, M)),
            out((8, 8, CASES)),
        ]
        + [out(shape) for shape in faces],
        scratch_shapes=[pltpu.VMEM((SPECIES, 48, M), BF16), pltpu.VMEM((M, M), BF16)],
        compiler_params=params(),
        cost_estimate=cost(1e9, 20e6),
        name="prep",
    )(row, column, flux, gap, load.reshape(SPECIES, 1, CASES))


def shifted(value, f):
    row = lax.broadcasted_iota(jnp.int32, value.shape, 0)
    zpos = row % NLAY
    ypos = (row // NLAY) % YCOLS
    xpos = row // (NLAY * YCOLS)
    step, ok = (
        (NLAY * YCOLS, xpos > 0),
        (-NLAY * YCOLS, xpos < NCOL // YCOLS - 1),
        (NLAY, ypos > 0),
        (-NLAY, ypos < YCOLS - 1),
        (1, zpos > 0),
        (-1, zpos < NLAY - 1),
    )[f]
    return jnp.where(ok, pltpu.roll(value, step % COUNT, 0), 0.0)


def own_half(value, lay):
    return jnp.where(lay % 2 == 0, value, pltpu.roll(value, HALF, value.ndim - 1))


def packed(first, second):
    lane = lax.broadcasted_iota(jnp.int32, first.shape, first.ndim - 1)
    return jnp.where(lane < HALF, first, pltpu.roll(second, HALF, second.ndim - 1))


def mid0_kernel(info_ref, got_ref, out_ref):
    lay = info_ref[1]

    def rows(r):
        return jnp.concatenate([got_ref[l, r : r + 1, :] for l in range(NLAY)], axis=0)

    halves = [own_half(rows(r), lay) for r in range(7)] + [rows(7)]
    tiles = [packed(halves[r], halves[r + 4]) for r in range(4)]
    for c in range(NCOL):
        for r in range(4):
            out_ref[c, r] = tiles[r]


def mid0(info, got):
    return pl.pallas_call(
        mid0_kernel,
        in_specs=[SMEM, pl.BlockSpec(memory_space=pltpu.VMEM)],
        out_specs=pl.BlockSpec(memory_space=pltpu.VMEM),
        out_shape=out((NCOL, 4, 8, CASES)),
        compiler_params=small(6),
        cost_estimate=cost(1e5, 6e5),
        name="pack_start",
    )(info, got)


def solve0_kernel(info_ref, inv_ref, gathered_ref, out_ref, vals_ref):
    col = info_ref[0]

    def rows(r):
        value = gathered_ref[:, r % 4].reshape(COUNT, CASES)
        return value if r < 4 else pltpu.roll(value, HALF, 1)

    inv = inv_ref[...]
    y0 = exact_dot(inv, rows(6), ((1,), (0,)))
    vals = [y0 - shifted(y0, f) for f in range(6)]
    rounded = [v.astype(BF16).astype(F32) for v in vals]
    table = rows(7)
    tau = []
    for f in range(6):
        total = rows(f)
        for g in range(6):
            total = total - table[:, 6 * f + g : 6 * f + g + 1] * rounded[g]
        tau.append(total)
    h = jnp.zeros((COUNT, CASES), F32)
    for f in range(6):
        h = h + (tau[f] - shifted(tau[f ^ 1], f))
    y1 = exact_dot(inv, h, ((1,), (0,)))
    here = pl.ds(pl.multiple_of(col * NLAY, NLAY), NLAY)
    zero = jnp.zeros((NLAY, CASES), F32)
    for f in range(6):
        vals_ref[0] = y1 - shifted(y1, f)
        out_ref[:, f, :] = vals_ref[0, here, :]
    for f in range(6):
        vals_ref[f] = vals[f]
    for g in range(6):
        out_ref[:, 8 + g, :] = vals_ref[g, here, :]
    for f in range(4):
        away = jnp.clip(col + (-YCOLS, YCOLS, -1, 1)[f], 0, NCOL - 1)
        there = pl.ds(pl.multiple_of(away * NLAY, NLAY), NLAY)
        for g in range(6):
            out_ref[:, 16 + 8 * f + g, :] = vals_ref[g, there, :]
    for f in (4, 5):
        for g in range(6):
            out_ref[:, 16 + 8 * f + g, :] = pltpu.roll(
                vals_ref[g, here, :], (1, NLAY - 1)[f - 4], 0
            )
    for group in range(8):
        out_ref[:, 8 * group + 6, :] = zero
        out_ref[:, 8 * group + 7, :] = zero


def solve0(info, inverse, gathered):
    return pl.pallas_call(
        solve0_kernel,
        in_specs=[SMEM, pl.BlockSpec(memory_space=pltpu.VMEM), pl.BlockSpec(memory_space=pltpu.VMEM)],
        out_specs=pl.BlockSpec(memory_space=pltpu.VMEM),
        out_shape=out((8, 64, CASES)),
        scratch_shapes=[pltpu.VMEM((6, COUNT, CASES), F32)],
        compiler_params=small(16),
        cost_estimate=cost(1e8, 2e6),
        name="solve_start",
    )(info, inverse, gathered)


def mid_kernel(info_ref, got_ref, out_ref):
    lay = info_ref[1]
    total = got_ref[0]
    top = got_ref[0, 5:6, :]
    for l in range(1, NLAY):
        total = total + got_ref[l]
        top = jnp.maximum(top, got_ref[l, 5:6, :])
    qq = jnp.zeros((1, CASES), F32)
    for l in range(NLAY):
        part = got_ref[l, 5:6, :] / top
        qq = qq + got_ref[l, 2:3, :] * (part * part)
    heads = [got_ref[l, 0:1, :] for l in range(NLAY)]
    zero = jnp.zeros((1, CASES), F32)
    first = jnp.concatenate(heads[:4] + [total[1:2], total[3:4], top, zero], axis=0)
    second = jnp.concatenate(heads[4:] + [qq, total[4:5], top, zero], axis=0)
    tile = packed(own_half(first, lay), own_half(second, lay))
    for c in range(NCOL):
        out_ref[c] = tile


def mid(info, got):
    return pl.pallas_call(
        mid_kernel,
        in_specs=[SMEM, pl.BlockSpec(memory_space=pltpu.VMEM)],
        out_specs=pl.BlockSpec(memory_space=pltpu.VMEM),
        out_shape=out((NCOL, 8, CASES)),
        compiler_params=small(4),
        cost_estimate=cost(1e5, 3e5),
        name="combine_layers",
    )(info, got)


def last_kernel(got_ref, out_ref):
    total = got_ref[0]
    for l in range(1, NLAY):
        total = total + got_ref[l]
    for c in range(NCOL):
        out_ref[c] = total


def last_mid(got):
    return pl.pallas_call(
        last_kernel,
        in_specs=[pl.BlockSpec(memory_space=pltpu.VMEM)],
        out_specs=pl.BlockSpec(memory_space=pltpu.VMEM),
        out_shape=out((NCOL, 8, CASES)),
        compiler_params=small(4),
        cost_estimate=cost(1e5, 3e5),
        name="combine_last",
    )(got)


def solve_kernel(info_ref, inv_ref, gathered_ref, out_ref, y_ref):
    col = info_ref[0]
    tiles = gathered_ref[...].reshape(COUNT, CASES)
    upper = pltpu.roll(tiles, HALF, 1)
    row = lax.broadcasted_iota(jnp.int32, (COUNT, CASES), 0) % 8
    tops = jnp.where(row == 6, tiles, 0.0)
    top = jnp.max(tops, axis=0, keepdims=True)
    part = pltpu.roll(tops, COUNT - 2, 0) / top
    qq = jnp.sum(jnp.where(row == 4, upper * (part * part), 0.0), axis=0, keepdims=True)
    pq = jnp.sum(jnp.where(row == 4, tiles, 0.0), axis=0, keepdims=True)
    wq = jnp.sum(jnp.where(row == 5, tiles, 0.0), axis=0, keepdims=True)
    energy = jnp.sum(jnp.where(row == 5, upper, 0.0), axis=0, keepdims=True)
    h = jnp.where(row < 4, tiles, pltpu.roll(upper, 4, 0)) / top
    y = exact_dot(inv_ref[...], h, ((1,), (0,)))
    hy = jnp.sum(h * y, axis=0, keepdims=True)
    alpha = energy / pq
    scaled = alpha * top
    new = energy - 2.0 * (alpha * wq) + (scaled * scaled) * (qq - hy)
    beta = new / energy
    y = y * top
    here = pl.ds(pl.multiple_of(col * NLAY, NLAY), NLAY)
    for f in range(6):
        y_ref[...] = y - shifted(y, f)
        out_ref[:, f, :] = y_ref[here, :]
    out_ref[:, 6, :] = jnp.broadcast_to(alpha, (NLAY, CASES))
    out_ref[:, 7, :] = jnp.broadcast_to(beta, (NLAY, CASES))


def solve(info, inverse, gathered):
    return pl.pallas_call(
        solve_kernel,
        in_specs=[SMEM, pl.BlockSpec(memory_space=pltpu.VMEM), pl.BlockSpec(memory_space=pltpu.VMEM)],
        out_specs=pl.BlockSpec(memory_space=pltpu.VMEM),
        out_shape=out((8, 8, CASES)),
        scratch_shapes=[pltpu.VMEM((COUNT, CASES), F32)],
        compiler_params=small(6),
        cost_estimate=cost(1e8, 1e6),
        name="solve_step",
    )(info, inverse, gathered)


ANY = pl.BlockSpec(memory_space=pl.ANY)
SCRATCH = [
    pltpu.VMEM((M, SPECIES * CASES), BF16),
    pltpu.VMEM((M, 2 * SPECIES * CASES), BF16),
    pltpu.VMEM((M, M), BF16),
    pltpu.VMEM((M, M), BF16),
    pltpu.VMEM((SPECIES, M, M), BF16),
    pltpu.SemaphoreType.DMA((SPECIES,)),
]


def fetches(flux_ref, scratch):
    flux_vmem, sems = scratch[4:]
    return [
        pltpu.make_async_copy(flux_ref.at[k], flux_vmem.at[k], sems.at[k])
        for k in range(SPECIES)
    ]


def store_direction(k, value, scratch):
    for s in range(SPECIES):

        @pl.when(k == s)
        def _():
            scratch[0][:, s * CASES : (s + 1) * CASES] = value.astype(BF16)


def apply_all(row_ref, col_ref, copies, scratch):
    x_ref, both_ref, o_vmem, ot_vmem, flux_vmem, _ = scratch
    wide = SPECIES * CASES
    fill_gather(col_ref, o_vmem)
    x_ref[...] = jnp.dot(o_vmem[...], x_ref[...], preferred_element_type=F32).astype(BF16)
    fill_scatter(row_ref, ot_vmem)
    for k in range(SPECIES):
        here = slice(k * CASES, (k + 1) * CASES)
        copies[k].wait()
        image = jnp.dot(flux_vmem[k], x_ref[:, here], preferred_element_type=F32)
        high = image.astype(BF16)
        both_ref[:, here] = high
        both_ref[:, wide + k * CASES : wide + (k + 1) * CASES] = (
            image - high.astype(F32)
        ).astype(BF16)


def moved_back(scratch, start, size):
    both_ref, ot_vmem = scratch[1], scratch[3]
    wide = SPECIES * CASES
    both = jnp.dot(ot_vmem[start : start + size, :], both_ref[...], preferred_element_type=F32)
    return both[:, :wide] + both[:, wide:]


def store_faces(scratch, faces):
    for first in (0, 2, 4):
        begin = STARTS[first]
        image = moved_back(scratch, begin, SIZES[first] + SIZES[first + 1])
        for f in (first, first + 1):
            offset = STARTS[f] - begin
            for k in range(SPECIES):
                faces[f][k] = image[offset : offset + SIZES[f], k * CASES : (k + 1) * CASES]


def merged(ref):
    lane = lax.broadcasted_iota(jnp.int32, ref.shape[1:], 1)
    return jnp.where(lane < HALF, ref[0], pltpu.roll(ref[1], HALF, 1))


def turned_dot(rt, values):
    left = jnp.concatenate(split3(rt), axis=0).astype(BF16)
    right = jnp.concatenate([values] * 3, axis=0).astype(BF16)
    return lax.dot_general(left, right, (((0,), (0,)), ((), ())), preferred_element_type=F32)


def start_kernel(gap_ref, rt_ref, back_ref, row_ref, col_ref, flux_ref, *refs):
    arrived = refs[:6]
    p_ref = refs[6]
    faces = refs[7:13]
    scratch = refs[13:]
    k = pl.program_id(0)
    copies = fetches(flux_ref, scratch)

    @pl.when(k == 0)
    def _():
        for copy in copies:
            copy.start()

    @pl.when(k < SPECIES)
    def _():
        table = merged(back_ref)
        own = turned_dot(rt_ref[0], table[8:16])
        for f in range(6):
            start, size = STARTS[f], SIZES[f]
            theirs = table[16 + 8 * f : 24 + 8 * f]
            other = turned_dot(arrived[f][0, size : size + 8, :], theirs)
            if size > CASES:
                more = turned_dot(arrived[f][0, size + 8 : size + 16, :], theirs)
                other = jnp.concatenate([other, more[: size - CASES]], axis=0)
            resid = (gap_ref[0, start : start + size, :] - own[start : start + size]) - (
                arrived[f][0, :size, :] - other
            )
            p_ref[0, start : start + size, :] = resid - table[f : f + 1, :]
        store_direction(k, p_ref[0], scratch)

    @pl.when(k == SPECIES)
    def _():
        apply_all(row_ref, col_ref, copies, scratch)
        store_faces(scratch, faces)


VECTOR = (SPECIES, M, CASES)
FACES = [(SPECIES, size, CASES) for size in SIZES]


def start(gap, rt, back, row, column, flux, arrived):
    return pl.pallas_call(
        start_kernel,
        grid=(SPECIES + 1,),
        in_specs=[
            per_species(M, CASES),
            per_species(8, M),
            pair(64, CASES),
            whole(1, M),
            whole(M, 1),
            ANY,
        ]
        + [per_species(SIZES[f] + TAILS[f], CASES) for f in range(6)],
        out_specs=[per_species(M, CASES)] + [whole(*shape) for shape in FACES],
        out_shape=[out(VECTOR)] + [out(shape) for shape in FACES],
        scratch_shapes=SCRATCH,
        compiler_params=params(),
        cost_estimate=cost(4e9, 20e6),
        name="start",
    )(gap, rt, back, row, column, flux, *arrived)


def weights(info_ref):
    col, lay = info_ref[0], info_ref[1]
    xpos, ypos = col // YCOLS, col % YCOLS
    flags = [
        xpos > 0,
        xpos < NCOL // YCOLS - 1,
        ypos > 0,
        ypos < YCOLS - 1,
        lay > 0,
        lay < NLAY - 1,
    ]
    return [jnp.where(flag, 0.5, 1.0).astype(F32) for flag in flags]


def dots_kernel(same, info_ref, *refs):
    count = 1 if same else 2
    p_ref = refs[0]
    w_ref = refs[count - 1]
    faces = refs[count : count + 6]
    arrived = refs[count + 6 : count + 12]
    q_ref, msg_ref = refs[count + 12 :]
    weight = weights(info_ref)
    top = jnp.zeros((1, CASES), F32)
    for f in range(6):
        q = faces[f][0] - arrived[f][0]
        q_ref[0, STARTS[f] : STARTS[f] + SIZES[f], :] = q
        top = jnp.maximum(top, jnp.max(jnp.abs(q), axis=0, keepdims=True))
    top = jnp.where(top > 0.0, top, 1e-30)
    head, pq, qq, wq, ww = [jnp.zeros((1, CASES), F32) for _ in range(5)]

    def total(value):
        return jnp.sum(value, axis=0, keepdims=True)

    for f in range(6):
        here = slice(STARTS[f], STARTS[f] + SIZES[f])
        q = q_ref[0, here, :]
        p = p_ref[0, here, :]
        unit = q / top
        head = head + total(q)
        pq = pq + weight[f] * total(p * q)
        qq = qq + weight[f] * total(unit * unit)
        if same:
            ww = ww + weight[f] * total(p * p)
        else:
            w = w_ref[0, here, :]
            wq = wq + weight[f] * total(w * q)
            ww = ww + weight[f] * total(w * w)
    if same:
        wq = pq
    zero = jnp.zeros((1, CASES), F32)
    rows = (head, pq, qq, wq, ww, top, zero, zero)
    for r in range(8):
        msg_ref[0, r : r + 1, :] = rows[r]
        msg_ref[1, r : r + 1, :] = rows[r]


def dots(info, vectors, faces, arrived):
    same = len(vectors) == 1
    return pl.pallas_call(
        functools.partial(dots_kernel, same),
        grid=(SPECIES,),
        in_specs=[SMEM]
        + [per_species(M, CASES)] * len(vectors)
        + [per_species(s, CASES) for s in SIZES] * 2,
        out_specs=[per_species(M, CASES), pair(8, CASES)],
        out_shape=[out(VECTOR), out((8, 8, CASES))],
        compiler_params=params(16 * MIB),
        cost_estimate=cost(1e7, 10e6),
        name="dots",
    )(info, *vectors, *faces, *arrived)


def step_kernel(same, last, info_ref, back_ref, row_ref, col_ref, flux_ref, *refs):
    count = 1 if same else 2
    p_ref = refs[0]
    w_ref = refs[count - 1]
    q_ref = refs[count]
    outs = refs[count + 1 : -len(SCRATCH) - 1]
    scratch = refs[-len(SCRATCH) - 1 : -1]
    held_ref = refs[-1]
    k = pl.program_id(0)
    copies = fetches(flux_ref, scratch)

    @pl.when(k == 0)
    def _():
        for copy in copies:
            copy.start()

    @pl.when(k < SPECIES)
    def _():
        table = merged(back_ref)
        alpha, beta = table[6:7], table[7:8]
        weight = weights(info_ref)
        ww = jnp.zeros((1, CASES), F32)
        for f in range(6):
            here = slice(STARTS[f], STARTS[f] + SIZES[f])
            w = w_ref[0, here, :] - alpha * (q_ref[0, here, :] - table[f : f + 1, :])
            if last:
                ww = ww + weight[f] * jnp.sum(w * w, axis=0, keepdims=True)
            else:
                outs[1][0, here, :] = w
            outs[0][0, here, :] = w + beta * p_ref[0, here, :]
        store_direction(k, outs[0][0], scratch)
        if last:
            held_ref[k] = outs[0][0]
            row = lax.broadcasted_iota(jnp.int32, (NLAY, 8, CASES), 1)
            outs[1][...] = jnp.where(row == k + SPECIES, ww[None], outs[1][...])

    @pl.when(k == SPECIES)
    def _():
        apply_all(row_ref, col_ref, copies, scratch)
        if not last:
            store_faces(scratch, outs[2:])
            return
        sums = [jnp.zeros((1, CASES), F32) for _ in range(SPECIES)]
        for i in range(0, M, M // 2):
            image = moved_back(scratch, i, M // 2)
            for s in range(SPECIES):
                part = held_ref[s, i : i + M // 2] * image[:, s * CASES : (s + 1) * CASES]
                sums[s] = sums[s] + jnp.sum(part, axis=0, keepdims=True)
        for s in range(SPECIES):
            pq = sums[s]
            for l in range(NLAY):
                outs[1][l, s : s + 1, :] = pq


def step(info, back, row, column, flux, vectors, q, last):
    same = len(vectors) == 1
    out_specs = [per_species(M, CASES)]
    out_shape = [out(VECTOR)]
    if last:
        out_specs += [whole(NLAY, 8, CASES)]
        out_shape += [out((NLAY, 8, CASES))]
    else:
        out_specs += [per_species(M, CASES)] + [whole(*shape) for shape in FACES]
        out_shape += [out(VECTOR)] + [out(shape) for shape in FACES]
    held = pltpu.VMEM(VECTOR if last else (1, 8, CASES), F32)
    return pl.pallas_call(
        functools.partial(step_kernel, same, last),
        grid=(SPECIES + 1,),
        in_specs=[SMEM, pair(8, CASES), whole(1, M), whole(M, 1), ANY]
        + [per_species(M, CASES)] * (len(vectors) + 1),
        out_specs=out_specs,
        out_shape=out_shape,
        scratch_shapes=SCRATCH + [held],
        compiler_params=params(),
        cost_estimate=cost(4e9, 20e6),
        name="step",
    )(info, back, row, column, flux, *vectors, q)


def finish_kernel(first_ref, back0_ref, back1_ref, sums_ref, p0_ref, p1_ref, p2_ref, out_ref):
    k = pl.program_id(0)
    sums = jnp.sum(sums_ref[...], axis=0)
    row = lax.broadcasted_iota(jnp.int32, (8, CASES), 0)
    pq = jnp.sum(jnp.where(row == k, sums, 0.0), axis=0, keepdims=True)
    ww = jnp.sum(jnp.where(row == k + SPECIES, sums, 0.0), axis=0, keepdims=True)
    initial = merged(first_ref)
    alpha0 = merged(back0_ref)[6:7]
    alpha1 = merged(back1_ref)[6:7]
    alpha2 = ww / pq
    for f in range(6):
        here = slice(STARTS[f], STARTS[f] + SIZES[f])
        value = initial[8 + f : 9 + f] + alpha0 * p0_ref[0, here, :]
        value = value + alpha1 * p1_ref[0, here, :]
        out_ref[0, here, :] = value + alpha2 * p2_ref[0, here, :]


def finish(first, back0, back1, sums, p0, p1, p2):
    return pl.pallas_call(
        finish_kernel,
        grid=(SPECIES,),
        in_specs=[pair(64, CASES), pair(8, CASES), pair(8, CASES), whole(NCOL, 8, CASES)]
        + [per_species(M, CASES)] * 3,
        out_specs=per_species(M, CASES),
        out_shape=out(VECTOR),
        compiler_params=params(16 * MIB),
        cost_estimate=cost(1e7, 8e6),
        name="finish",
    )(first, back0, back1, sums, p0, p1, p2)


def exchange(blocks):
    def moved(value, axis, pairs):
        return lax.ppermute(value, axis, pairs)

    def along_x(step):
        return [(c, c + step) for c in range(NCOL) if 0 <= c + step < NCOL]

    def along_y(step):
        return [(c, c + step) for c in range(NCOL) if 0 <= c % YCOLS + step < YCOLS]

    def along_z(step):
        return [(l, l + step) for l in range(NLAY) if 0 <= l + step < NLAY]

    return [
        moved(blocks[1], "col", along_x(YCOLS)),
        moved(blocks[0], "col", along_x(-YCOLS)),
        moved(blocks[3], "col", along_y(1)),
        moved(blocks[2], "col", along_y(-1)),
        moved(blocks[5], "lay", along_z(1)),
        moved(blocks[4], "lay", along_z(-1)),
    ]


def swap(value, axis):
    return lax.all_to_all(value, axis, 0, 0, tiled=True)


def shards(flux_operator, dof_order, local_gap, rigid_load):
    flux = flux_operator[0, 0]
    order = dof_order[0, 0]
    gap = local_gap[0, 0]
    load = rigid_load[0, 0]
    info = jnp.stack([lax.axis_index("col"), lax.axis_index("lay")]).astype(jnp.int32)
    inverse = jnp.asarray(coarse_inverse())

    row, column = order.reshape(1, M), order.reshape(M, 1)
    rt, message, *faces = prep(row, column, flux, gap, load)
    arrived = exchange(faces)
    packed_start = mid0(info, swap(message, "lay"))
    back_first = swap(solve0(info, inverse, swap(packed_start, "col")), "lay")
    p0, *faces = start(gap, rt, back_first, row, column, flux, arrived)

    q, message = dots(info, [p0], faces, exchange(faces))
    gathered = swap(mid(info, swap(message, "lay")), "col")
    back0 = swap(solve(info, inverse, gathered), "lay")
    p1, w1, *faces = step(info, back0, row, column, flux, [p0], q, False)

    q, message = dots(info, [p1, w1], faces, exchange(faces))
    gathered = swap(mid(info, swap(message, "lay")), "col")
    back1 = swap(solve(info, inverse, gathered), "lay")
    p2, message = step(info, back1, row, column, flux, [p1, w1], q, True)

    sums = swap(last_mid(swap(message, "lay")), "col")
    return finish(back_first, back0, back1, sums, p0, p1, p2)[None, None]


def solution(mesh):
    return jax.shard_map(
        shards,
        mesh=mesh,
        in_specs=(
            P("col", "lay", None, None, None),
            P("col", "lay", None),
            P("col", "lay", None, None, None),
            P("col", "lay", None, None),
        ),
        out_specs=P("col", "lay", None, None, None),
        check_vma=False,
    )
```

```python
import functools

import jax
import jax.numpy as jnp
import numpy as np
from jax import lax
from jax.experimental import pallas as pl
from jax.experimental.pallas import tpu as pltpu
from jax.sharding import PartitionSpec as P

SIDE = 192
TOP = 128
YCOLS = 4
SPECIES = 4
CASES = 128
M = 1024
NCOL = 32
NLAY = 8
COUNT = NCOL * NLAY
SIZES = (SIDE, SIDE, SIDE, SIDE, TOP, TOP)
STARTS = (0, 192, 384, 576, 768, 896)
TAILS = (16, 16, 16, 16, 8, 8)
CHUNK = 256
HALF = CASES // 2
F32 = jnp.float32
BF16 = jnp.bfloat16
MIB = 1024 * 1024
VMEM_LIMIT = 40 * MIB


def coarse_inverse():
    index = np.arange(COUNT)
    zpos, cpos = index % NLAY, index // NLAY
    ypos, xpos = cpos % YCOLS, cpos // YCOLS
    dx = np.abs(xpos[:, None] - xpos[None, :])
    dy = np.abs(ypos[:, None] - ypos[None, :])
    dz = np.abs(zpos[:, None] - zpos[None, :])
    lateral = (dx + dy == 1) & (dz == 0)
    upward = (dx + dy == 0) & (dz == 1)
    matrix = M * np.eye(COUNT) - SIDE * lateral - TOP * upward
    return np.linalg.inv(matrix).astype(np.float32)


def params(limit=VMEM_LIMIT):
    return pltpu.CompilerParams(
        dimension_semantics=("arbitrary",), vmem_limit_bytes=limit
    )


def small(limit):
    return pltpu.CompilerParams(vmem_limit_bytes=limit * MIB)


def cost(flops, nbytes):
    return pl.CostEstimate(flops=int(flops), bytes_accessed=int(nbytes), transcendentals=0)


SMEM = pl.BlockSpec(memory_space=pltpu.SMEM)


def per_species(*shape):
    zeros = (0,) * len(shape)
    return pl.BlockSpec((1,) + shape, lambda k: (jnp.minimum(k, SPECIES - 1),) + zeros)


def whole(*shape):
    zeros = (0,) * len(shape)
    return pl.BlockSpec(shape, lambda k: zeros)


def pair(*shape):
    zeros = (0,) * len(shape)
    return pl.BlockSpec((2,) + shape, lambda k: (jnp.minimum(k, SPECIES - 1),) + zeros)


def out(shape, dtype=F32):
    return jax.ShapeDtypeStruct(shape, dtype)


def exact_dot(a, b, dims):
    return lax.dot_general(
        a, b, (dims, ((), ())), precision=lax.Precision.HIGHEST, preferred_element_type=F32
    )


def split3(value):
    first = value.astype(BF16).astype(F32)
    rest = value - first
    second = rest.astype(BF16).astype(F32)
    return [first, second, rest - second]


def fill_gather(col_ref, o_ref):
    lanes = lax.broadcasted_iota(jnp.int16, (CHUNK, M), 1)
    one, zero = jnp.ones((), BF16), jnp.zeros((), BF16)
    for i in range(0, M, CHUNK):
        hit = col_ref[i : i + CHUNK, :].astype(jnp.int16) == lanes
        o_ref[i : i + CHUNK, :] = jnp.where(hit, one, zero)


def fill_scatter(row_ref, ot_ref):
    row = jnp.broadcast_to(row_ref[...], (CHUNK, M)).astype(jnp.int16)
    index = lax.broadcasted_iota(jnp.int16, (CHUNK, M), 0)
    one, zero = jnp.ones((), BF16), jnp.zeros((), BF16)
    for i in range(0, M, CHUNK):
        hit = row == index + jnp.int16(i)
        ot_ref[i : i + CHUNK, :] = jnp.where(hit, one, zero)


def prep_kernel(row_ref, col_ref, flux_ref, gap_ref, load_ref, *refs):
    rt_ref, msg_ref = refs[:2]
    face_refs = refs[2:8]
    parts_ref, o_ref = refs[8:]
    k = pl.program_id(0)
    row = row_ref[...]

    face = lax.broadcasted_iota(jnp.int32, (16, M), 0)
    low = jnp.where(face <= 4, SIDE * face, jnp.where(face == 5, STARTS[5], M))
    high = jnp.where(face <= 3, SIDE * (face + 1), jnp.where(face == 4, STARTS[5], M))
    member = jnp.where((row >= low) & (row < high), 1.0, 0.0).astype(BF16)
    sums = jnp.dot(member, flux_ref[0], preferred_element_type=F32)
    for i, part in enumerate(split3(sums)):
        parts_ref[k, 16 * i : 16 * i + 16, :] = part.astype(BF16)
    rows = [
        jnp.sum(gap_ref[0, STARTS[f] : STARTS[f] + SIZES[f], :], axis=0, keepdims=True)
        for f in range(6)
    ]
    rows.append(load_ref[0])
    held = jnp.concatenate(rows + [jnp.zeros((1, CASES), F32)], axis=0)
    msg_ref[2 * k] = held
    msg_ref[2 * k + 1] = held
    for f in range(6):
        face_refs[f][k, : SIZES[f], :] = gap_ref[0, STARTS[f] : STARTS[f] + SIZES[f], :]

    @pl.when(k == SPECIES - 1)
    def _():
        fill_gather(col_ref, o_ref)
        parts = parts_ref[...].reshape(SPECIES * 48, M)
        moved = jnp.dot(parts, o_ref[...], preferred_element_type=F32)
        lane = lax.broadcasted_iota(jnp.int32, (8, M), 1)
        slot = lax.broadcasted_iota(jnp.int32, (8, CASES), 1)
        peer = lax.broadcasted_iota(jnp.int32, (8, CASES), 0)
        for s in range(SPECIES):
            base = 48 * s
            rt = moved[base : base + 8] + moved[base + 16 : base + 24]
            rt = rt + moved[base + 32 : base + 40]
            rt_ref[s] = rt
            table = jnp.zeros((8, CASES), F32)
            for f in range(6):
                inside = (lane >= STARTS[f]) & (lane < STARTS[f] + SIZES[f])
                total = jnp.sum(jnp.where(inside, rt, 0.0), axis=1, keepdims=True)
                here = (slot == 6 * f + peer) & (peer < 6)
                table = table + jnp.where(here, total, 0.0)
            table = jnp.sum(table, axis=0, keepdims=True)
            msg_ref[2 * s, 7:8, :] = table
            msg_ref[2 * s + 1, 7:8, :] = table
            for f in range(6):
                size = SIZES[f]
                turned = rt if STARTS[f] == 0 else pltpu.roll(rt, M - STARTS[f], 1)
                face_refs[f][s, size : size + 8, :] = turned[:, :CASES]
                if size > CASES:
                    face_refs[f][s, size + 8 : size + 16, :] = turned[:, CASES : 2 * CASES]


def prep(row, column, flux, gap, load):
    faces = [(SPECIES, SIZES[f] + TAILS[f], CASES) for f in range(6)]
    return pl.pallas_call(
        prep_kernel,
        grid=(SPECIES,),
        in_specs=[
            whole(1, M),
            whole(M, 1),
            per_species(M, M),
            per_species(M, CASES),
            per_species(1, CASES),
        ],
        out_specs=[whole(SPECIES, 8, M), whole(8, 8, CASES)]
        + [whole(*shape) for shape in faces],
        out_shape=[
            out((SPECIES, 8, M)),
            out((8, 8, CASES)),
        ]
        + [out(shape) for shape in faces],
        scratch_shapes=[pltpu.VMEM((SPECIES, 48, M), BF16), pltpu.VMEM((M, M), BF16)],
        compiler_params=params(60 * MIB),
        cost_estimate=cost(1e9, 20e6),
        name="prep",
    )(row, column, flux, gap, load.reshape(SPECIES, 1, CASES))


def shifted(value, f):
    row = lax.broadcasted_iota(jnp.int32, value.shape, 0)
    zpos = row % NLAY
    ypos = (row // NLAY) % YCOLS
    xpos = row // (NLAY * YCOLS)
    step, ok = (
        (NLAY * YCOLS, xpos > 0),
        (-NLAY * YCOLS, xpos < NCOL // YCOLS - 1),
        (NLAY, ypos > 0),
        (-NLAY, ypos < YCOLS - 1),
        (1, zpos > 0),
        (-1, zpos < NLAY - 1),
    )[f]
    return jnp.where(ok, pltpu.roll(value, step % COUNT, 0), 0.0)


def own_half(value, lay):
    return jnp.where(lay % 2 == 0, value, pltpu.roll(value, HALF, value.ndim - 1))


def packed(first, second):
    lane = lax.broadcasted_iota(jnp.int32, first.shape, first.ndim - 1)
    return jnp.where(lane < HALF, first, pltpu.roll(second, HALF, second.ndim - 1))


def mid0_kernel(info_ref, got_ref, out_ref):
    lay = info_ref[1]

    def rows(r):
        return jnp.concatenate([got_ref[l, r : r + 1, :] for l in range(NLAY)], axis=0)

    halves = [own_half(rows(r), lay) for r in range(7)] + [rows(7)]
    tiles = [packed(halves[r], halves[r + 4]) for r in range(4)]
    for c in range(NCOL):
        for r in range(4):
            out_ref[c, r] = tiles[r]


def mid0(info, got):
    return pl.pallas_call(
        mid0_kernel,
        in_specs=[SMEM, pl.BlockSpec(memory_space=pltpu.VMEM)],
        out_specs=pl.BlockSpec(memory_space=pltpu.VMEM),
        out_shape=out((NCOL, 4, 8, CASES)),
        compiler_params=small(6),
        cost_estimate=cost(1e5, 6e5),
        name="pack_start",
    )(info, got)


def solve0_kernel(info_ref, inv_ref, gathered_ref, out_ref, vals_ref):
    col = info_ref[0]

    def rows(r):
        value = gathered_ref[:, r % 4].reshape(COUNT, CASES)
        return value if r < 4 else pltpu.roll(value, HALF, 1)

    inv = inv_ref[...]
    y0 = exact_dot(inv, rows(6), ((1,), (0,)))
    vals = [y0 - shifted(y0, f) for f in range(6)]
    rounded = [v.astype(BF16).astype(F32) for v in vals]
    table = rows(7)
    tau = []
    for f in range(6):
        total = rows(f)
        for g in range(6):
            total = total - table[:, 6 * f + g : 6 * f + g + 1] * rounded[g]
        tau.append(total)
    h = jnp.zeros((COUNT, CASES), F32)
    for f in range(6):
        h = h + (tau[f] - shifted(tau[f ^ 1], f))
    y1 = exact_dot(inv, h, ((1,), (0,)))
    here = pl.ds(pl.multiple_of(col * NLAY, NLAY), NLAY)
    zero = jnp.zeros((NLAY, CASES), F32)
    for f in range(6):
        vals_ref[0] = y1 - shifted(y1, f)
        out_ref[:, f, :] = vals_ref[0, here, :]
    for f in range(6):
        vals_ref[f] = vals[f]
    for g in range(6):
        out_ref[:, 8 + g, :] = vals_ref[g, here, :]
    for f in range(4):
        away = jnp.clip(col + (-YCOLS, YCOLS, -1, 1)[f], 0, NCOL - 1)
        there = pl.ds(pl.multiple_of(away * NLAY, NLAY), NLAY)
        for g in range(6):
            out_ref[:, 16 + 8 * f + g, :] = vals_ref[g, there, :]
    for f in (4, 5):
        for g in range(6):
            out_ref[:, 16 + 8 * f + g, :] = pltpu.roll(
                vals_ref[g, here, :], (1, NLAY - 1)[f - 4], 0
            )
    for group in range(8):
        out_ref[:, 8 * group + 6, :] = zero
        out_ref[:, 8 * group + 7, :] = zero


def solve0(info, inverse, gathered):
    return pl.pallas_call(
        solve0_kernel,
        in_specs=[SMEM, pl.BlockSpec(memory_space=pltpu.VMEM), pl.BlockSpec(memory_space=pltpu.VMEM)],
        out_specs=pl.BlockSpec(memory_space=pltpu.VMEM),
        out_shape=out((8, 64, CASES)),
        scratch_shapes=[pltpu.VMEM((6, COUNT, CASES), F32)],
        compiler_params=small(16),
        cost_estimate=cost(1e8, 2e6),
        name="solve_start",
    )(info, inverse, gathered)


def mid_kernel(info_ref, got_ref, out_ref):
    lay = info_ref[1]
    total = got_ref[0]
    top = got_ref[0, 5:6, :]
    for l in range(1, NLAY):
        total = total + got_ref[l]
        top = jnp.maximum(top, got_ref[l, 5:6, :])
    qq = jnp.zeros((1, CASES), F32)
    for l in range(NLAY):
        part = got_ref[l, 5:6, :] / top
        qq = qq + got_ref[l, 2:3, :] * (part * part)
    heads = [got_ref[l, 0:1, :] for l in range(NLAY)]
    zero = jnp.zeros((1, CASES), F32)
    first = jnp.concatenate(heads[:4] + [total[1:2], total[3:4], top, zero], axis=0)
    second = jnp.concatenate(heads[4:] + [qq, total[4:5], top, zero], axis=0)
    tile = packed(own_half(first, lay), own_half(second, lay))
    for c in range(NCOL):
        out_ref[c] = tile


def mid(info, got):
    return pl.pallas_call(
        mid_kernel,
        in_specs=[SMEM, pl.BlockSpec(memory_space=pltpu.VMEM)],
        out_specs=pl.BlockSpec(memory_space=pltpu.VMEM),
        out_shape=out((NCOL, 8, CASES)),
        compiler_params=small(4),
        cost_estimate=cost(1e5, 3e5),
        name="combine_layers",
    )(info, got)


def last_kernel(got_ref, out_ref):
    total = got_ref[0]
    for l in range(1, NLAY):
        total = total + got_ref[l]
    for c in range(NCOL):
        out_ref[c] = total


def last_mid(got):
    return pl.pallas_call(
        last_kernel,
        in_specs=[pl.BlockSpec(memory_space=pltpu.VMEM)],
        out_specs=pl.BlockSpec(memory_space=pltpu.VMEM),
        out_shape=out((NCOL, 8, CASES)),
        compiler_params=small(4),
        cost_estimate=cost(1e5, 3e5),
        name="combine_last",
    )(got)


def solve_kernel(info_ref, inv_ref, gathered_ref, out_ref, y_ref):
    col = info_ref[0]
    tiles = gathered_ref[...].reshape(COUNT, CASES)
    upper = pltpu.roll(tiles, HALF, 1)
    row = lax.broadcasted_iota(jnp.int32, (COUNT, CASES), 0) % 8
    tops = jnp.where(row == 6, tiles, 0.0)
    top = jnp.max(tops, axis=0, keepdims=True)
    part = pltpu.roll(tops, COUNT - 2, 0) / top
    qq = jnp.sum(jnp.where(row == 4, upper * (part * part), 0.0), axis=0, keepdims=True)
    pq = jnp.sum(jnp.where(row == 4, tiles, 0.0), axis=0, keepdims=True)
    wq = jnp.sum(jnp.where(row == 5, tiles, 0.0), axis=0, keepdims=True)
    energy = jnp.sum(jnp.where(row == 5, upper, 0.0), axis=0, keepdims=True)
    h = jnp.where(row < 4, tiles, pltpu.roll(upper, 4, 0)) / top
    y = exact_dot(inv_ref[...], h, ((1,), (0,)))
    hy = jnp.sum(h * y, axis=0, keepdims=True)
    alpha = energy / pq
    scaled = alpha * top
    new = energy - 2.0 * (alpha * wq) + (scaled * scaled) * (qq - hy)
    beta = new / energy
    y = y * top
    here = pl.ds(pl.multiple_of(col * NLAY, NLAY), NLAY)
    for f in range(6):
        y_ref[...] = y - shifted(y, f)
        out_ref[:, f, :] = y_ref[here, :]
    out_ref[:, 6, :] = jnp.broadcast_to(alpha, (NLAY, CASES))
    out_ref[:, 7, :] = jnp.broadcast_to(beta, (NLAY, CASES))


def solve(info, inverse, gathered):
    return pl.pallas_call(
        solve_kernel,
        in_specs=[SMEM, pl.BlockSpec(memory_space=pltpu.VMEM), pl.BlockSpec(memory_space=pltpu.VMEM)],
        out_specs=pl.BlockSpec(memory_space=pltpu.VMEM),
        out_shape=out((8, 8, CASES)),
        scratch_shapes=[pltpu.VMEM((COUNT, CASES), F32)],
        compiler_params=small(6),
        cost_estimate=cost(1e8, 1e6),
        name="solve_step",
    )(info, inverse, gathered)


ANY = pl.BlockSpec(memory_space=pl.ANY)
SCRATCH = [
    pltpu.VMEM((M, SPECIES * CASES), BF16),
    pltpu.VMEM((M, 2 * SPECIES * CASES), BF16),
    pltpu.VMEM((M, M), BF16),
    pltpu.VMEM((M, M), BF16),
    pltpu.VMEM((SPECIES, M, M), BF16),
    pltpu.SemaphoreType.DMA((SPECIES,)),
]


def fetches(flux_ref, scratch):
    flux_vmem, sems = scratch[4:]
    return [
        pltpu.make_async_copy(flux_ref.at[k], flux_vmem.at[k], sems.at[k])
        for k in range(SPECIES)
    ]


def store_direction(k, value, scratch):
    for s in range(SPECIES):

        @pl.when(k == s)
        def _():
            scratch[0][:, s * CASES : (s + 1) * CASES] = value.astype(BF16)


def apply_all(row_ref, col_ref, copies, scratch):
    x_ref, both_ref, o_vmem, ot_vmem, flux_vmem, _ = scratch
    wide = SPECIES * CASES
    fill_gather(col_ref, o_vmem)
    x_ref[...] = jnp.dot(o_vmem[...], x_ref[...], preferred_element_type=F32).astype(BF16)
    fill_scatter(row_ref, ot_vmem)
    for k in range(SPECIES):
        here = slice(k * CASES, (k + 1) * CASES)
        copies[k].wait()
        image = jnp.dot(flux_vmem[k], x_ref[:, here], preferred_element_type=F32)
        high = image.astype(BF16)
        both_ref[:, here] = high
        both_ref[:, wide + k * CASES : wide + (k + 1) * CASES] = (
            image - high.astype(F32)
        ).astype(BF16)


def moved_back(scratch, start, size):
    both_ref, ot_vmem = scratch[1], scratch[3]
    wide = SPECIES * CASES
    both = jnp.dot(ot_vmem[start : start + size, :], both_ref[...], preferred_element_type=F32)
    return both[:, :wide] + both[:, wide:]


def store_faces(scratch, faces):
    for first in (0, 2, 4):
        begin = STARTS[first]
        image = moved_back(scratch, begin, SIZES[first] + SIZES[first + 1])
        for f in (first, first + 1):
            offset = STARTS[f] - begin
            for k in range(SPECIES):
                faces[f][k] = image[offset : offset + SIZES[f], k * CASES : (k + 1) * CASES]


def merged(ref):
    lane = lax.broadcasted_iota(jnp.int32, ref.shape[1:], 1)
    return jnp.where(lane < HALF, ref[0], pltpu.roll(ref[1], HALF, 1))


def turned_dot(rt, values):
    left = jnp.concatenate(split3(rt), axis=0).astype(BF16)
    right = jnp.concatenate([values] * 3, axis=0).astype(BF16)
    return lax.dot_general(left, right, (((0,), (0,)), ((), ())), preferred_element_type=F32)


def start_kernel(gap_ref, rt_ref, back_ref, row_ref, col_ref, flux_ref, *refs):
    arrived = refs[:6]
    p_ref = refs[6]
    faces = refs[7:13]
    scratch = refs[13:]
    k = pl.program_id(0)
    copies = fetches(flux_ref, scratch)

    @pl.when(k == 0)
    def _():
        for copy in copies:
            copy.start()

    @pl.when(k < SPECIES)
    def _():
        table = merged(back_ref)
        own = turned_dot(rt_ref[0], table[8:16])
        for f in range(6):
            start, size = STARTS[f], SIZES[f]
            theirs = table[16 + 8 * f : 24 + 8 * f]
            other = turned_dot(arrived[f][0, size : size + 8, :], theirs)
            if size > CASES:
                more = turned_dot(arrived[f][0, size + 8 : size + 16, :], theirs)
                other = jnp.concatenate([other, more[: size - CASES]], axis=0)
            resid = (gap_ref[0, start : start + size, :] - own[start : start + size]) - (
                arrived[f][0, :size, :] - other
            )
            p_ref[0, start : start + size, :] = resid - table[f : f + 1, :]
        store_direction(k, p_ref[0], scratch)

    @pl.when(k == SPECIES)
    def _():
        apply_all(row_ref, col_ref, copies, scratch)
        store_faces(scratch, faces)


VECTOR = (SPECIES, M, CASES)
FACES = [(SPECIES, size, CASES) for size in SIZES]


def start(gap, rt, back, row, column, flux, arrived):
    return pl.pallas_call(
        start_kernel,
        grid=(SPECIES + 1,),
        in_specs=[
            per_species(M, CASES),
            per_species(8, M),
            pair(64, CASES),
            whole(1, M),
            whole(M, 1),
            ANY,
        ]
        + [per_species(SIZES[f] + TAILS[f], CASES) for f in range(6)],
        out_specs=[per_species(M, CASES)] + [whole(*shape) for shape in FACES],
        out_shape=[out(VECTOR)] + [out(shape) for shape in FACES],
        scratch_shapes=SCRATCH,
        compiler_params=params(),
        cost_estimate=cost(4e9, 20e6),
        name="start",
    )(gap, rt, back, row, column, flux, *arrived)


def weights(info_ref):
    col, lay = info_ref[0], info_ref[1]
    xpos, ypos = col // YCOLS, col % YCOLS
    flags = [
        xpos > 0,
        xpos < NCOL // YCOLS - 1,
        ypos > 0,
        ypos < YCOLS - 1,
        lay > 0,
        lay < NLAY - 1,
    ]
    return [jnp.where(flag, 0.5, 1.0).astype(F32) for flag in flags]


def dots_kernel(same, info_ref, *refs):
    count = 1 if same else 2
    p_ref = refs[0]
    w_ref = refs[count - 1]
    faces = refs[count : count + 6]
    arrived = refs[count + 6 : count + 12]
    q_ref, msg_ref = refs[count + 12 :]
    weight = weights(info_ref)
    top = jnp.zeros((1, CASES), F32)
    for f in range(6):
        q = faces[f][0] - arrived[f][0]
        q_ref[0, STARTS[f] : STARTS[f] + SIZES[f], :] = q
        top = jnp.maximum(top, jnp.max(jnp.abs(q), axis=0, keepdims=True))
    top = jnp.where(top > 0.0, top, 1e-30)
    head, pq, qq, wq, ww = [jnp.zeros((1, CASES), F32) for _ in range(5)]

    def total(value):
        return jnp.sum(value, axis=0, keepdims=True)

    for f in range(6):
        here = slice(STARTS[f], STARTS[f] + SIZES[f])
        q = q_ref[0, here, :]
        p = p_ref[0, here, :]
        unit = q / top
        head = head + total(q)
        pq = pq + weight[f] * total(p * q)
        qq = qq + weight[f] * total(unit * unit)
        if same:
            ww = ww + weight[f] * total(p * p)
        else:
            w = w_ref[0, here, :]
            wq = wq + weight[f] * total(w * q)
            ww = ww + weight[f] * total(w * w)
    if same:
        wq = pq
    zero = jnp.zeros((1, CASES), F32)
    rows = (head, pq, qq, wq, ww, top, zero, zero)
    for r in range(8):
        msg_ref[0, r : r + 1, :] = rows[r]
        msg_ref[1, r : r + 1, :] = rows[r]


def dots(info, vectors, faces, arrived):
    same = len(vectors) == 1
    return pl.pallas_call(
        functools.partial(dots_kernel, same),
        grid=(SPECIES,),
        in_specs=[SMEM]
        + [per_species(M, CASES)] * len(vectors)
        + [per_species(s, CASES) for s in SIZES] * 2,
        out_specs=[per_species(M, CASES), pair(8, CASES)],
        out_shape=[out(VECTOR), out((8, 8, CASES))],
        compiler_params=params(16 * MIB),
        cost_estimate=cost(1e7, 10e6),
        name="dots",
    )(info, *vectors, *faces, *arrived)


def step_kernel(same, last, info_ref, back_ref, row_ref, col_ref, flux_ref, *refs):
    count = 1 if same else 2
    p_ref = refs[0]
    w_ref = refs[count - 1]
    q_ref = refs[count]
    outs = refs[count + 1 : -len(SCRATCH) - 1]
    scratch = refs[-len(SCRATCH) - 1 : -1]
    held_ref = refs[-1]
    k = pl.program_id(0)
    copies = fetches(flux_ref, scratch)

    @pl.when(k == 0)
    def _():
        for copy in copies:
            copy.start()

    @pl.when(k < SPECIES)
    def _():
        table = merged(back_ref)
        alpha, beta = table[6:7], table[7:8]
        weight = weights(info_ref)
        ww = jnp.zeros((1, CASES), F32)
        for f in range(6):
            here = slice(STARTS[f], STARTS[f] + SIZES[f])
            w = w_ref[0, here, :] - alpha * (q_ref[0, here, :] - table[f : f + 1, :])
            if last:
                ww = ww + weight[f] * jnp.sum(w * w, axis=0, keepdims=True)
            else:
                outs[1][0, here, :] = w
            outs[0][0, here, :] = w + beta * p_ref[0, here, :]
        store_direction(k, outs[0][0], scratch)
        if last:
            held_ref[k] = outs[0][0]
            row = lax.broadcasted_iota(jnp.int32, (NLAY, 8, CASES), 1)
            outs[1][...] = jnp.where(row == k + SPECIES, ww[None], outs[1][...])

    @pl.when(k == SPECIES)
    def _():
        apply_all(row_ref, col_ref, copies, scratch)
        if not last:
            store_faces(scratch, outs[2:])
            return
        sums = [jnp.zeros((1, CASES), F32) for _ in range(SPECIES)]
        for i in range(0, M, M // 2):
            image = moved_back(scratch, i, M // 2)
            for s in range(SPECIES):
                part = held_ref[s, i : i + M // 2] * image[:, s * CASES : (s + 1) * CASES]
                sums[s] = sums[s] + jnp.sum(part, axis=0, keepdims=True)
        for s in range(SPECIES):
            pq = sums[s]
            for l in range(NLAY):
                outs[1][l, s : s + 1, :] = pq


def step(info, back, row, column, flux, vectors, q, last):
    same = len(vectors) == 1
    out_specs = [per_species(M, CASES)]
    out_shape = [out(VECTOR)]
    if last:
        out_specs += [whole(NLAY, 8, CASES)]
        out_shape += [out((NLAY, 8, CASES))]
    else:
        out_specs += [per_species(M, CASES)] + [whole(*shape) for shape in FACES]
        out_shape += [out(VECTOR)] + [out(shape) for shape in FACES]
    held = pltpu.VMEM(VECTOR if last else (1, 8, CASES), F32)
    return pl.pallas_call(
        functools.partial(step_kernel, same, last),
        grid=(SPECIES + 1,),
        in_specs=[SMEM, pair(8, CASES), whole(1, M), whole(M, 1), ANY]
        + [per_species(M, CASES)] * (len(vectors) + 1),
        out_specs=out_specs,
        out_shape=out_shape,
        scratch_shapes=SCRATCH + [held],
        compiler_params=params(),
        cost_estimate=cost(4e9, 20e6),
        name="step",
    )(info, back, row, column, flux, *vectors, q)


def finish_kernel(first_ref, back0_ref, back1_ref, sums_ref, p0_ref, p1_ref, p2_ref, out_ref):
    k = pl.program_id(0)
    sums = jnp.sum(sums_ref[...], axis=0)
    row = lax.broadcasted_iota(jnp.int32, (8, CASES), 0)
    pq = jnp.sum(jnp.where(row == k, sums, 0.0), axis=0, keepdims=True)
    ww = jnp.sum(jnp.where(row == k + SPECIES, sums, 0.0), axis=0, keepdims=True)
    initial = merged(first_ref)
    alpha0 = merged(back0_ref)[6:7]
    alpha1 = merged(back1_ref)[6:7]
    alpha2 = ww / pq
    for f in range(6):
        here = slice(STARTS[f], STARTS[f] + SIZES[f])
        value = initial[8 + f : 9 + f] + alpha0 * p0_ref[0, here, :]
        value = value + alpha1 * p1_ref[0, here, :]
        out_ref[0, here, :] = value + alpha2 * p2_ref[0, here, :]


def finish(first, back0, back1, sums, p0, p1, p2):
    return pl.pallas_call(
        finish_kernel,
        grid=(SPECIES,),
        in_specs=[pair(64, CASES), pair(8, CASES), pair(8, CASES), whole(NCOL, 8, CASES)]
        + [per_species(M, CASES)] * 3,
        out_specs=per_species(M, CASES),
        out_shape=out(VECTOR),
        compiler_params=params(16 * MIB),
        cost_estimate=cost(1e7, 8e6),
        name="finish",
    )(first, back0, back1, sums, p0, p1, p2)


def exchange(blocks):
    def moved(value, axis, pairs):
        return lax.ppermute(value, axis, pairs)

    def along_x(step):
        return [(c, c + step) for c in range(NCOL) if 0 <= c + step < NCOL]

    def along_y(step):
        return [(c, c + step) for c in range(NCOL) if 0 <= c % YCOLS + step < YCOLS]

    def along_z(step):
        return [(l, l + step) for l in range(NLAY) if 0 <= l + step < NLAY]

    return [
        moved(blocks[1], "col", along_x(YCOLS)),
        moved(blocks[0], "col", along_x(-YCOLS)),
        moved(blocks[3], "col", along_y(1)),
        moved(blocks[2], "col", along_y(-1)),
        moved(blocks[5], "lay", along_z(1)),
        moved(blocks[4], "lay", along_z(-1)),
    ]


def swap(value, axis):
    return lax.all_to_all(value, axis, 0, 0, tiled=True)


def shards(flux_operator, dof_order, local_gap, rigid_load):
    flux = flux_operator[0, 0]
    order = dof_order[0, 0]
    gap = local_gap[0, 0]
    load = rigid_load[0, 0]
    info = jnp.stack([lax.axis_index("col"), lax.axis_index("lay")]).astype(jnp.int32)
    inverse = jnp.asarray(coarse_inverse())

    row, column = order.reshape(1, M), order.reshape(M, 1)
    rt, message, *faces = prep(row, column, flux, gap, load)
    arrived = exchange(faces)
    packed_start = mid0(info, swap(message, "lay"))
    back_first = swap(solve0(info, inverse, swap(packed_start, "col")), "lay")
    p0, *faces = start(gap, rt, back_first, row, column, flux, arrived)

    q, message = dots(info, [p0], faces, exchange(faces))
    gathered = swap(mid(info, swap(message, "lay")), "col")
    back0 = swap(solve(info, inverse, gathered), "lay")
    p1, w1, *faces = step(info, back0, row, column, flux, [p0], q, False)

    q, message = dots(info, [p1, w1], faces, exchange(faces))
    gathered = swap(mid(info, swap(message, "lay")), "col")
    back1 = swap(solve(info, inverse, gathered), "lay")
    p2, message = step(info, back1, row, column, flux, [p1, w1], q, True)

    sums = swap(last_mid(swap(message, "lay")), "col")
    return finish(back_first, back0, back1, sums, p0, p1, p2)[None, None]


def solution(mesh):
    return jax.shard_map(
        shards,
        mesh=mesh,
        in_specs=(
            P("col", "lay", None, None, None),
            P("col", "lay", None),
            P("col", "lay", None, None, None),
            P("col", "lay", None, None),
        ),
        out_specs=P("col", "lay", None, None, None),
        check_vma=False,
    )
```
